32 devices in a mesh: pipe: 2 (over x), ctx: 16 (over z, y, core).
Axes of the slice: x: 2, y: 2, z: 4, core: 2. Of those that a mesh axis runs over, the one named last changes fastest.
Arguments:
- saved_in: bfloat16 [2, 2048, 2048], P('pipe', 'ctx'), may hold values from -20 to 20, as said below
- grad_in: bfloat16 [2, 2048, 2048], P('pipe', 'ctx'), may hold values from -6 to 6
- queries: bfloat16 [2, 2048, 2048], P('pipe', 'ctx'), may hold values from -60 to 60
- d_heads: bfloat16 [2, 2048, 2048], P('pipe', 'ctx'), may hold values from -6 to 6
- kv_weights: bfloat16 [2, 2048, 512], P('pipe', 'ctx'), may hold values from -0.125 to 0.125
Outputs:
- grad_out: bfloat16 [2, 2048, 2048], P('pipe', 'ctx')
- d_queries: bfloat16 [2, 2048, 2048], P('pipe', 'ctx')
- weight_grad: float32 [2, 2048, 512], P('pipe', 'ctx')
The draws below stay inside these ranges and needn't reach their ends.
Inputs may be any that keep to these rules, and one draw needn't show every extreme that they name: `saved_in`: stored layer activations.
All inputs are finite; a program needn't handle non-finite values.
Results may differ from the reference program's by a relative error of at most 0.0039.
The reference program's roundings to bfloat16 on the way count: a program that leaves them out, or rounds other values in their place, can miss the bound.
Values may be sent and summed in bfloat16 or wider, within the bound.
No kernel may reach another device: no remote copies, remote signals or barrier semaphores. Data moves between devices by JAX's collectives and lax.ppermute only.
A program may use at most 64 MiB of HBM per device.

```python
import math
import jax
import jax.numpy as jnp
from jax import lax

D = 2048
HEADS = 16
HEAD_DIM = 128
KV_HEADS = 2
TOK_DEV = 128
KV_WIDTH = 256
SECTIONS = 2
TOKENS = 2048
N_CTX = 16


def draw_saved_in(key, part):
    shape = (SECTIONS, TOKENS, D)
    base_key = jax.random.fold_in(jax.random.fold_in(key, 11), 0)
    return jnp.clip(jax.random.normal(base_key, shape, jnp.float32), -4.0, 4.0).astype(jnp.bfloat16)


def draw_queries(key, part):
    shape = (SECTIONS, TOKENS, D)
    base_key = jax.random.fold_in(jax.random.fold_in(key, 23), 0)
    values = jnp.clip(jax.random.normal(base_key, shape, jnp.float32), -4.0, 4.0)
    return values.astype(jnp.bfloat16)


def block_levels(stream_key, dims, cuts, least, largest):
    loudness = 1.0
    for dim, blocks in cuts:
        steps = jax.random.uniform(jax.random.fold_in(jax.random.fold_in(stream_key, 6), dim), (blocks,), jnp.float32, least / len(cuts), largest / len(cuts))
        loudness = loudness * jnp.repeat(jnp.exp(steps), dims[dim] // blocks).reshape((-1,) + (1,) * (len(dims) - 1 - dim))
    return loudness


def gaussian(key, shape, width, most, pieces=(), dtype=jnp.bfloat16):
    result = jax.random.normal(key, shape, jnp.float32) * width
    if len(pieces) > 0:
        result = block_levels(key, shape, pieces, -0.22, 0.18) * result
    return jnp.clip(result, min=-most, max=most).astype(dtype)


def setup_inputs(seed: int = 0) -> dict:
    key_of = jax.random.split(jax.random.key(seed), 6)
    saved_in = draw_saved_in(jax.random.fold_in(key_of[5], 71), 0)
    grad_in = gaussian(key_of[1], (SECTIONS, TOKENS, D), 1.0, 6.0, ((0, 2), (1, 16)))
    queries = draw_queries(jax.random.fold_in(key_of[5], 71), 0)
    d_heads = gaussian(key_of[3], (SECTIONS, TOKENS, D), 1.0, 6.0, ((0, 2), (1, 16)))
    kv_weights = gaussian(key_of[4], (SECTIONS, D, 2 * KV_WIDTH), D ** -0.5, 0.125, ((0, 2), (1, 16)))
    return {"saved_in": saved_in, "grad_in": grad_in, "queries": queries, "d_heads": d_heads, "kv_weights": kv_weights}


epsilon = 1e-06

def neighbours(blocks):
    return jnp.concatenate([jnp.roll(blocks, 1, axis=0), blocks, jnp.roll(blocks, -1, axis=0)], axis=1)

def fold_back(wide_rows):
    lower = wide_rows[:, :TOK_DEV]
    middle = wide_rows[:, TOK_DEV:2 * TOK_DEV]
    upper = wide_rows[:, 2 * TOK_DEV:]
    return middle + jnp.roll(lower, -1, axis=0) + jnp.roll(upper, 1, axis=0)

def window_mask(row_count):
    query_pos = lax.broadcasted_iota(jnp.int32, (row_count, 3 * row_count), 0)
    key_pos = lax.broadcasted_iota(jnp.int32, (row_count, 3 * row_count), 1)
    offset = key_pos - query_pos
    return (offset >= 0) & (offset <= 2 * row_count)

def section_pass(saved, upstream, query_in, grad_heads, kv_matrix):
    per_group = HEADS // KV_HEADS
    score_scale = 1.0 / math.sqrt(HEAD_DIM)
    highest = lax.Precision.HIGHEST
    blocks = saved.reshape(N_CTX, TOK_DEV, D).astype(jnp.float32)
    factor = lax.rsqrt(lax.optimization_barrier(jnp.mean(blocks * blocks, axis=-1, keepdims=True)) + epsilon)
    normed = blocks * factor
    normed_b = normed.astype(jnp.bfloat16)
    flat_b = normed_b.reshape(TOKENS, D)
    kv_rows = jnp.dot(flat_b, kv_matrix, preferred_element_type=jnp.float32).astype(jnp.bfloat16)
    kv_rows = kv_rows.reshape(N_CTX, TOK_DEV, 2 * KV_WIDTH)
    key_rows = neighbours(kv_rows[..., :KV_WIDTH]).reshape(N_CTX, 3 * TOK_DEV, KV_HEADS, HEAD_DIM).astype(jnp.float32)
    value_rows = neighbours(kv_rows[..., KV_WIDTH:]).reshape(N_CTX, 3 * TOK_DEV, KV_HEADS, HEAD_DIM).astype(jnp.float32)
    query_rows = query_in.reshape(N_CTX, TOK_DEV, KV_HEADS, per_group, HEAD_DIM).astype(jnp.float32)
    grad_rows = grad_heads.reshape(N_CTX, TOK_DEV, KV_HEADS, per_group, HEAD_DIM).astype(jnp.float32)
    scores = jnp.einsum('bqgne,bkge->bgnqk', query_rows, key_rows) * score_scale
    scores = jnp.where(window_mask(TOK_DEV)[None, None, None], scores, -1e+30)
    row_peak = lax.optimization_barrier(jnp.max(scores, axis=-1, keepdims=True))
    lifted = jnp.exp(scores - row_peak)
    probs = lifted / lax.optimization_barrier(jnp.sum(lifted, axis=-1, keepdims=True))
    probs_b = probs.astype(jnp.bfloat16).astype(jnp.float32)
    d_probs = jnp.einsum('bqgne,bkge->bgnqk', grad_rows, value_rows)
    row_dot = lax.optimization_barrier(jnp.sum(probs * d_probs, axis=-1, keepdims=True))
    d_scores = (probs * (d_probs - row_dot) * score_scale).astype(jnp.bfloat16).astype(jnp.float32)
    d_queries = jnp.einsum('bgnqk,bkge->bqgne', d_scores, key_rows).astype(jnp.bfloat16).reshape(TOKENS, D)
    d_key_wide = jnp.einsum('bgnqk,bqgne->bkge', d_scores, query_rows).reshape(N_CTX, 3 * TOK_DEV, KV_WIDTH)
    d_value_wide = jnp.einsum('bgnqk,bqgne->bkge', probs_b, grad_rows).reshape(N_CTX, 3 * TOK_DEV, KV_WIDTH)
    d_kv = jnp.concatenate([fold_back(d_key_wide), fold_back(d_value_wide)], axis=-1).reshape(TOKENS, 2 * KV_WIDTH)
    d_normed = jnp.dot(d_kv, kv_matrix.astype(jnp.float32).T, precision=highest).reshape(N_CTX, TOK_DEV, D)
    upstream_wide = upstream.reshape(N_CTX, TOK_DEV, D).astype(jnp.float32)
    grad_out = (upstream_wide + factor * (d_normed - normed * lax.optimization_barrier(jnp.mean(d_normed * normed, axis=-1, keepdims=True)))).astype(jnp.bfloat16)
    weight_grad = jnp.dot(flat_b.astype(jnp.float32).T, d_kv, precision=highest) * (1.0 / math.sqrt(TOKENS))
    return (grad_out.reshape(TOKENS, D), d_queries, weight_grad)

def reference(saved_in, grad_in, queries, d_heads, kv_weights):
    grad_outs = []
    query_grads = []
    weight_grads = []
    for section in range(SECTIONS):
        upstream = grad_in[(section + 1) % SECTIONS]
        grad_out, d_queries, weight_grad = section_pass(saved_in[section], upstream, queries[section], d_heads[section], kv_weights[section])
        grad_outs.append(grad_out)
        query_grads.append(d_queries)
        weight_grads.append(weight_grad)
    return (jnp.stack(grad_outs), jnp.stack(query_grads), jnp.stack(weight_grads))
```

```python
import functools
import math

import jax
import jax.numpy as jnp
from jax import lax
from jax.experimental import pallas as pl
from jax.experimental.pallas import tpu as pltpu
from jax.sharding import PartitionSpec as P

HEAD_DIM = 128
KV_HEADS = 2
EPSILON = 1e-06
NT = (((1,), (1,)), ((), ()))
VMEM = pl.BlockSpec(memory_space=pltpu.VMEM)
SMEM = pl.BlockSpec(memory_space=pltpu.SMEM)
PARAMS = pltpu.CompilerParams(vmem_limit_bytes=48 * 1024 * 1024)


def f32dot(a, b, dims=(((1,), (0,)), ((), ()))):
    return lax.dot_general(a, b, dims, preferred_element_type=jnp.float32)


def call(kernel, outs, args, scratch=()):
    in_specs = [SMEM if a.dtype == jnp.int32 else VMEM for a in args]
    return pl.pallas_call(
        kernel,
        out_shape=[jax.ShapeDtypeStruct(s, d) for s, d in outs],
        in_specs=in_specs,
        out_specs=[VMEM] * len(outs),
        scratch_shapes=list(scratch),
        compiler_params=PARAMS,
    )(*args)


def norm_kernel(me_ref, saved_ref, *refs):
    plain, turned = refs[:4], refs[4:8]
    factor_ref, held, held_t = refs[8:]
    blocks, _, width = held.shape
    rest = me_ref[0] % 4
    wide = saved_ref[...].astype(jnp.float32)
    factor = lax.rsqrt(jnp.mean(wide * wide, axis=-1, keepdims=True) + EPSILON)
    factor_ref[...] = factor
    normed = (wide * factor).astype(jnp.bfloat16)
    for b in range(blocks):
        part = normed[:, b * width : (b + 1) * width]
        held[b] = part
        held_t[b] = part.T
    for d in range(4):
        for zz in range(blocks // 4):
            source = zz * 4 + (rest ^ d)
            plain[d][zz] = held[source]
            turned[d][zz] = held_t[source]


def kv_kernel(me_ref, *refs):
    plain, weights, out_ref = refs[:4], refs[4:-1], refs[-1]
    own = me_ref[0] // 4
    total = None
    for delta, weight in enumerate(weights):
        part = f32dot(plain[delta % 4][own ^ (delta // 4)], weight[...])
        total = part if total is None else total + part
    out_ref[...] = total.astype(jnp.bfloat16)


def attention_kernel(q_ref, g_ref, lower_ref, own_ref, upper_ref, dq_ref, dl_ref, do_ref, du_ref):
    rows, model = q_ref.shape
    dim = HEAD_DIM
    kv_width = KV_HEADS * dim
    per_group = model // kv_width
    scale = 1.0 / math.sqrt(dim)
    key_pos = lax.broadcasted_iota(jnp.int32, (rows, rows), 0)
    query_pos = lax.broadcasted_iota(jnp.int32, (rows, rows), 1)
    first = jnp.concatenate([key_pos >= query_pos] * 2, axis=1)
    last = jnp.concatenate([key_pos <= query_pos] * 2, axis=1)
    for group in range(KV_HEADS):
        at = group * dim
        keys = jnp.concatenate([r[:, at : at + dim] for r in (lower_ref, own_ref, upper_ref)], axis=0)
        at += kv_width
        values = jnp.concatenate([r[:, at : at + dim] for r in (lower_ref, own_ref, upper_ref)], axis=0)
        keys_t = keys.T
        d_keys = d_values = None
        for pair in range(per_group // 2):
            h = (group * per_group + 2 * pair) * dim
            q = jnp.concatenate([q_ref[:, h : h + dim], q_ref[:, h + dim : h + 2 * dim]], axis=0)
            g = jnp.concatenate([g_ref[:, h : h + dim], g_ref[:, h + dim : h + 2 * dim]], axis=0)
            scores = f32dot(keys, q, NT) * scale
            scores = jnp.concatenate(
                [
                    jnp.where(first, scores[:rows], -1e30),
                    scores[rows : 2 * rows],
                    jnp.where(last, scores[2 * rows :], -1e30),
                ],
                axis=0,
            )
            lifted = jnp.exp(scores - jnp.max(scores, axis=0, keepdims=True))
            probs = lifted * (1.0 / jnp.sum(lifted, axis=0, keepdims=True))
            d_probs = f32dot(values, g, NT)
            weighted = probs * d_probs
            row_dot = jnp.sum(weighted, axis=0, keepdims=True)
            d_scores = ((weighted - probs * row_dot) * scale).astype(jnp.bfloat16)
            probs_b = probs.astype(jnp.bfloat16)
            dk = f32dot(d_scores, q)
            dv = f32dot(probs_b, g)
            d_keys = dk if d_keys is None else d_keys + dk
            d_values = dv if d_values is None else d_values + dv
            dq = f32dot(keys_t, d_scores).astype(jnp.bfloat16)
            dq_ref[:, h : h + dim] = dq[:, :rows].T
            dq_ref[:, h + dim : h + 2 * dim] = dq[:, rows:].T
        for at, grad in ((group * dim, d_keys), (kv_width + group * dim, d_values)):
            dl_ref[:, at : at + dim] = grad[:rows].astype(jnp.bfloat16)
            do_ref[:, at : at + dim] = grad[rows : 2 * rows]
            du_ref[:, at : at + dim] = grad[2 * rows :].astype(jnp.bfloat16)


def terms_kernel(me_ref, *refs):
    turned, grads, outs = refs[:4], refs[4:8], refs[8:]
    own = me_ref[0] // 4
    d_kv = jnp.concatenate([r[...] for r in grads], axis=0)
    for delta, out_ref in enumerate(outs):
        lhs = jnp.concatenate([t[own ^ delta] for t in turned], axis=1)
        out_ref[...] = f32dot(lhs, d_kv).astype(out_ref.dtype)


def input_kernel(me_ref, saved_ref, factor_ref, up_ref, do_ref, a_ref, b_ref, *refs):
    weights, out_ref, held = refs[:-2], refs[-2], refs[-1]
    blocks, rows, width = held.shape
    d_kv = do_ref[...] + a_ref[...].astype(jnp.float32) + b_ref[...].astype(jnp.float32)
    high = d_kv.astype(jnp.bfloat16)
    low = (d_kv - high.astype(jnp.float32)).astype(jnp.bfloat16)
    both = jnp.concatenate([high, low], axis=0)
    for delta, weight in enumerate(weights):
        part = f32dot(both, weight[...], NT)
        held[me_ref[0] ^ delta] = part[:rows] + part[rows:]
    factor = factor_ref[...]
    acc = jnp.zeros((rows, width), jnp.float32)
    for b in range(blocks):
        normed = saved_ref[:, b * width : (b + 1) * width].astype(jnp.float32) * factor
        acc = acc + held[b] * normed
    mean = jnp.sum(acc, axis=-1, keepdims=True) * (1.0 / (blocks * width))
    for b in range(blocks):
        at = slice(b * width, (b + 1) * width)
        normed = saved_ref[:, at].astype(jnp.float32) * factor
        grad = up_ref[:, at].astype(jnp.float32) + factor * (held[b] - normed * mean)
        out_ref[:, at] = grad.astype(jnp.bfloat16)


def swap(block, distance):
    count = lax.axis_size("ctx")
    return lax.ppermute(block, "ctx", [(i, i ^ distance) for i in range(count)])


def shifted(block, axis, distance):
    count = lax.axis_size(axis)
    return lax.ppermute(block, axis, [((i - distance) % count, i) for i in range(count)])


def gathered(block):
    count = lax.axis_size("ctx")
    parts = {0: block}
    step = count // 2
    while step >= 4:
        parts.update({d ^ step: swap(p, step) for d, p in list(parts.items())})
        step //= 2
    parts.update({d ^ 2: swap(p, 2) for d, p in list(parts.items())})
    parts.update({d ^ 1: swap(p, 1) for d, p in list(parts.items())})
    return [parts[d] for d in range(count)]


def per_device(saved_in, grad_in, queries, d_heads, kv_weights):
    count = lax.axis_size("ctx")
    me = lax.axis_index("ctx").astype(jnp.int32).reshape(1)
    bf16, f32 = jnp.bfloat16, jnp.float32
    saved = saved_in[0]
    rows, model = saved.shape
    width, kv2 = kv_weights.shape[1:]
    tall = count // 4
    weights = gathered(kv_weights[0])
    upstream = shifted(grad_in, "pipe", -1)[0]
    pieces = call(
        norm_kernel,
        [((tall, rows, width), bf16)] * 4 + [((tall, width, rows), bf16)] * 4 + [((rows, 1), f32)],
        [me, saved],
        [pltpu.VMEM((count, rows, width), bf16), pltpu.VMEM((count, width, rows), bf16)],
    )
    plain, turned, factor = pieces[:4], pieces[4:8], pieces[8]
    turned = [turned[0]] + [swap(turned[d], d) for d in (1, 2, 3)]
    (kv,) = call(kv_kernel, [((rows, kv2), bf16)], [me, *plain, *weights])
    kv_lower = shifted(kv, "ctx", 1)
    kv_upper = shifted(kv, "ctx", -1)
    half = ((rows, kv2), bf16)
    d_queries, d_lower, d_own, d_upper = call(
        attention_kernel,
        [((rows, model), bf16), half, ((rows, kv2), f32), half],
        [queries[0], d_heads[0], kv_lower, kv, kv_upper],
    )
    from_upper = shifted(d_lower, "ctx", -1)
    from_lower = shifted(d_upper, "ctx", 1)
    d_kv = (d_own + from_upper.astype(f32) + from_lower.astype(f32)).astype(bf16)
    beside = swap(d_kv, 1)
    across = swap(d_kv, 2)
    grads = [d_kv, beside, across, swap(across, 1)]
    terms = call(
        terms_kernel,
        [((width, kv2), f32)] + [((width, kv2), bf16)] * (tall - 1),
        [me, *turned, *grads],
    )
    total = terms[0]
    for delta in range(1, tall):
        total = total + swap(terms[delta], 4 * delta).astype(f32)
    weight_grad = total * (1.0 / math.sqrt(rows * count))
    (grad_out,) = call(
        input_kernel,
        [((rows, model), bf16)],
        [me, saved, factor, upstream, d_own, from_upper, from_lower, *weights],
        [pltpu.VMEM((count, rows, width), f32)],
    )
    return (grad_out[None], d_queries[None], weight_grad[None])


def solution(mesh):
    spec = P("pipe", "ctx", None)
    return jax.shard_map(
        per_device, mesh=mesh, in_specs=(spec,) * 5, out_specs=(spec,) * 3, check_vma=False
    )
```

```python
import functools
import math

import jax
import jax.numpy as jnp
from jax import lax
from jax.experimental import pallas as pl
from jax.experimental.pallas import tpu as pltpu
from jax.sharding import PartitionSpec as P

HEAD_DIM = 128
KV_HEADS = 2
EPSILON = 1e-06
NT = (((1,), (1,)), ((), ()))
VMEM = pl.BlockSpec(memory_space=pltpu.VMEM)
SMEM = pl.BlockSpec(memory_space=pltpu.SMEM)
PARAMS = pltpu.CompilerParams(vmem_limit_bytes=48 * 1024 * 1024)


def f32dot(a, b, dims=(((1,), (0,)), ((), ()))):
    return lax.dot_general(a, b, dims, preferred_element_type=jnp.float32)


def call(kernel, outs, args, scratch=()):
    in_specs = [SMEM if a.dtype == jnp.int32 else VMEM for a in args]
    return pl.pallas_call(
        kernel,
        out_shape=[jax.ShapeDtypeStruct(s, d) for s, d in outs],
        in_specs=in_specs,
        out_specs=[VMEM] * len(outs),
        scratch_shapes=list(scratch),
        compiler_params=PARAMS,
    )(*args)


def norm_kernel(me_ref, saved_ref, *refs):
    plain, turned = refs[:4], refs[4:8]
    factor_ref, held, held_t = refs[8:]
    blocks, _, width = held.shape
    rest = me_ref[0] % 4
    wide = saved_ref[...].astype(jnp.float32)
    factor = lax.rsqrt(jnp.mean(wide * wide, axis=-1, keepdims=True) + EPSILON)
    factor_ref[...] = factor
    normed = (wide * factor).astype(jnp.bfloat16)
    for b in range(blocks):
        part = normed[:, b * width : (b + 1) * width]
        held[b] = part
        held_t[b] = part.T
    for d in range(4):
        for zz in range(blocks // 4):
            source = zz * 4 + (rest ^ d)
            plain[d][zz] = held[source]
            turned[d][zz] = held_t[source]


def kv_kernel(me_ref, *refs):
    plain, weights, out_ref = refs[:4], refs[4:-1], refs[-1]
    own = me_ref[0] // 4
    total = None
    for delta, weight in enumerate(weights):
        part = f32dot(plain[delta % 4][own ^ (delta // 4)], weight[...])
        total = part if total is None else total + part
    out_ref[...] = total.astype(jnp.bfloat16)


def attention_kernel(me_ref, q_ref, g_ref, own_ref, beside_ref, across_ref, dq_ref, db_ref, do_ref, da_ref):
    rows, model = q_ref.shape
    dim = HEAD_DIM
    kv_width = KV_HEADS * dim
    per_group = model // kv_width
    scale = 1.0 / math.sqrt(dim)
    key_pos = lax.broadcasted_iota(jnp.int32, (rows, rows), 0)
    query_pos = lax.broadcasted_iota(jnp.int32, (rows, rows), 1)
    offset = (key_pos - query_pos) * (1 - 2 * (me_ref[0] % 2))
    beside_mask = jnp.concatenate([offset <= 0] * 2, axis=1)
    across_mask = jnp.concatenate([offset >= 0] * 2, axis=1)
    parts = (beside_ref, own_ref, across_ref)
    for group in range(KV_HEADS):
        at = group * dim
        keys = jnp.concatenate([r[:, at : at + dim] for r in parts], axis=0)
        at += kv_width
        values = jnp.concatenate([r[:, at : at + dim] for r in parts], axis=0)
        keys_t = keys.T
        d_keys = d_values = None
        for pair in range(per_group // 2):
            h = (group * per_group + 2 * pair) * dim
            q = jnp.concatenate([q_ref[:, h : h + dim], q_ref[:, h + dim : h + 2 * dim]], axis=0)
            g = jnp.concatenate([g_ref[:, h : h + dim], g_ref[:, h + dim : h + 2 * dim]], axis=0)
            scores = f32dot(keys, q, NT) * scale
            scores = jnp.concatenate(
                [
                    jnp.where(beside_mask, scores[:rows], -1e30),
                    scores[rows : 2 * rows],
                    jnp.where(across_mask, scores[2 * rows :], -1e30),
                ],
                axis=0,
            )
            lifted = jnp.exp(scores - jnp.max(scores, axis=0, keepdims=True))
            probs = lifted * (1.0 / jnp.sum(lifted, axis=0, keepdims=True))
            d_probs = f32dot(values, g, NT)
            weighted = probs * d_probs
            row_dot = jnp.sum(weighted, axis=0, keepdims=True)
            d_scores = ((weighted - probs * row_dot) * scale).astype(jnp.bfloat16)
            probs_b = probs.astype(jnp.bfloat16)
            dk = f32dot(d_scores, q)
            dv = f32dot(probs_b, g)
            d_keys = dk if d_keys is None else d_keys + dk
            d_values = dv if d_values is None else d_values + dv
            dq = f32dot(keys_t, d_scores).astype(jnp.bfloat16)
            dq_ref[:, h : h + dim] = dq[:, :rows].T
            dq_ref[:, h + dim : h + 2 * dim] = dq[:, rows:].T
        for at, grad in ((group * dim, d_keys), (kv_width + group * dim, d_values)):
            db_ref[:, at : at + dim] = grad[:rows].astype(jnp.bfloat16)
            do_ref[:, at : at + dim] = grad[rows : 2 * rows]
            da_ref[:, at : at + dim] = grad[2 * rows :].astype(jnp.bfloat16)


def terms_kernel(me_ref, *refs):
    turned, grads, outs = refs[:4], refs[4:8], refs[8:]
    own = me_ref[0] // 4
    d_kv = jnp.concatenate([r[...] for r in grads], axis=0)
    for delta, out_ref in enumerate(outs):
        lhs = jnp.concatenate([t[own ^ delta] for t in turned], axis=1)
        out_ref[...] = f32dot(lhs, d_kv).astype(out_ref.dtype)


def input_kernel(me_ref, saved_ref, factor_ref, up_ref, do_ref, a_ref, b_ref, *refs):
    weights, out_ref, held = refs[:-2], refs[-2], refs[-1]
    blocks, rows, width = held.shape
    d_kv = do_ref[...] + a_ref[...].astype(jnp.float32) + b_ref[...].astype(jnp.float32)
    high = d_kv.astype(jnp.bfloat16)
    low = (d_kv - high.astype(jnp.float32)).astype(jnp.bfloat16)
    both = jnp.concatenate([high, low], axis=0)
    for delta, weight in enumerate(weights):
        part = f32dot(both, weight[...], NT)
        held[me_ref[0] ^ delta] = part[:rows] + part[rows:]
    factor = factor_ref[...]
    acc = jnp.zeros((rows, width), jnp.float32)
    for b in range(blocks):
        normed = saved_ref[:, b * width : (b + 1) * width].astype(jnp.float32) * factor
        acc = acc + held[b] * normed
    mean = jnp.sum(acc, axis=-1, keepdims=True) * (1.0 / (blocks * width))
    for b in range(blocks):
        at = slice(b * width, (b + 1) * width)
        normed = saved_ref[:, at].astype(jnp.float32) * factor
        grad = up_ref[:, at].astype(jnp.float32) + factor * (held[b] - normed * mean)
        out_ref[:, at] = grad.astype(jnp.bfloat16)


def swap(block, distance):
    count = lax.axis_size("ctx")
    return lax.ppermute(block, "ctx", [(i, i ^ distance) for i in range(count)])


def shifted(block, axis, distance):
    count = lax.axis_size(axis)
    return lax.ppermute(block, axis, [((i - distance) % count, i) for i in range(count)])


def crossed(block):
    count = lax.axis_size("ctx")
    route = [(i, (i + 1) % count if i % 2 else (i - 1) % count) for i in range(count)]
    return lax.ppermute(block, "ctx", route)


def gathered(block, meanwhile):
    count = lax.axis_size("ctx")
    first = count // 2
    parts = {0: block, first: swap(block, first)}
    parts[2] = swap(block, 2)
    far = [0, first]
    step = first // 2
    while step >= 4:
        for d in list(far):
            parts[d ^ step] = swap(parts[d], step)
            far.append(d ^ step)
        step //= 2
    parts[first], meanwhile = lax.optimization_barrier((parts[first], meanwhile))
    for d in far[1:]:
        direct = d & (first | 4) == first | 4 and first > 4
        parts[d ^ 2] = swap(parts[d ^ 4], 6) if direct else swap(parts[d], 2)
    parts.update({d ^ 1: swap(p, 1) for d, p in list(parts.items())})
    return [parts[d] for d in range(count)], meanwhile


def per_device(saved_in, grad_in, queries, d_heads, kv_weights):
    count = lax.axis_size("ctx")
    me = lax.axis_index("ctx").astype(jnp.int32).reshape(1)
    bf16, f32 = jnp.bfloat16, jnp.float32
    saved = saved_in[0]
    rows, model = saved.shape
    width, kv2 = kv_weights.shape[1:]
    tall = count // 4
    pieces = call(
        norm_kernel,
        [((tall, rows, width), bf16)] * 4 + [((tall, width, rows), bf16)] * 4 + [((rows, 1), f32)],
        [me, saved],
        [pltpu.VMEM((count, rows, width), bf16), pltpu.VMEM((count, width, rows), bf16)],
    )
    weights, pieces = gathered(kv_weights[0], pieces)
    weights[8], grad_in = lax.optimization_barrier((weights[8], grad_in))
    upstream = shifted(grad_in, "pipe", -1)[0]
    plain, turned, factor = pieces[:4], pieces[4:8], pieces[8]
    turned = [turned[0]] + [swap(turned[d], d) for d in (1, 2, 3)]
    half = ((rows, kv2), bf16)
    (kv,) = call(kv_kernel, [half], [me, *plain, *weights])
    across = crossed(kv)
    beside = swap(kv, 1)
    d_queries, d_beside, d_own, d_across = call(
        attention_kernel,
        [((rows, model), bf16), half, ((rows, kv2), f32), half],
        [me, queries[0], d_heads[0], kv, beside, across],
    )
    d_across, turned, upstream = lax.optimization_barrier((d_across, turned, upstream))
    from_across = crossed(d_across)
    from_beside = swap(d_beside, 1)
    d_kv = (d_own + from_beside.astype(f32) + from_across.astype(f32)).astype(bf16)
    above = swap(d_kv, 2)
    grads = [d_kv, swap(d_kv, 1), above, swap(above, 1)]
    terms = call(
        terms_kernel,
        [((width, kv2), f32)] + [((width, kv2), bf16)] * (tall - 1),
        [me, *turned, *grads],
    )
    total = terms[0]
    for delta in reversed(range(1, tall)):
        total = total + swap(terms[delta], 4 * delta).astype(f32)
    weight_grad = total * (1.0 / math.sqrt(rows * count))
    (grad_out,) = call(
        input_kernel,
        [((rows, model), bf16)],
        [me, saved, factor, upstream, d_own, from_beside, from_across, *weights],
        [pltpu.VMEM((count, rows, width), f32)],
    )
    return (grad_out[None], d_queries[None], weight_grad[None])


def solution(mesh):
    spec = P("pipe", "ctx", None)
    return jax.shard_map(
        per_device, mesh=mesh, in_specs=(spec,) * 5, out_specs=(spec,) * 3, check_vma=False
    )
```

```python
import functools
import math

import jax
import jax.numpy as jnp
from jax import lax
from jax.experimental import pallas as pl
from jax.experimental.pallas import tpu as pltpu
from jax.sharding import PartitionSpec as P

HEAD_DIM = 128
KV_HEADS = 2
EPSILON = 1e-06
NT = (((1,), (1,)), ((), ()))
VMEM = pl.BlockSpec(memory_space=pltpu.VMEM)
SMEM = pl.BlockSpec(memory_space=pltpu.SMEM)
PARAMS = pltpu.CompilerParams(vmem_limit_bytes=16 * 1024 * 1024)


def f32dot(a, b, dims=(((1,), (0,)), ((), ()))):
    return lax.dot_general(a, b, dims, preferred_element_type=jnp.float32)


def call(kernel, outs, args, scratch=()):
    in_specs = [SMEM if a.dtype == jnp.int32 else VMEM for a in args]
    return pl.pallas_call(
        kernel,
        out_shape=[jax.ShapeDtypeStruct(s, d) for s, d in outs],
        in_specs=in_specs,
        out_specs=[VMEM] * len(outs),
        scratch_shapes=list(scratch),
        compiler_params=PARAMS,
    )(*args)


def norm_kernel(me_ref, saved_ref, shard_ref, near_ref, lent_ref, t0_ref, t2_ref, t3_ref, factor_ref, copy_ref, held, held_t):
    copy_ref[...] = shard_ref[...]
    blocks, _, width = held.shape
    rest = me_ref[0] % 4
    wide = saved_ref[...].astype(jnp.float32)
    factor = lax.rsqrt(jnp.mean(wide * wide, axis=-1, keepdims=True) + EPSILON)
    factor_ref[...] = factor
    normed = (wide * factor).astype(jnp.bfloat16)
    for b in range(blocks):
        part = normed[:, b * width : (b + 1) * width]
        held[b] = part
        held_t[b] = part.T
    for zz in range(blocks // 4):
        for k in range(2):
            near_ref[k, zz] = held[zz * 4 + (rest ^ (2 * k))]
            lent_ref[k, zz] = held[zz * 4 + (rest ^ (2 * k + 1))]
        for d, ref in ((0, t0_ref), (2, t2_ref), (3, t3_ref)):
            ref[zz] = held_t[zz * 4 + (rest ^ d)]


def kv_kernel(me_ref, near_ref, lent_ref, *refs):
    weights, own_ref, beside_ref = refs[:-2], refs[-2], refs[-1]
    own = me_ref[0] // 4
    rows = own_ref.shape[0]
    total = None
    for half, weight in enumerate(weights):
        at = own ^ (half // 2)
        lhs = jnp.concatenate([near_ref[half % 2, at], lent_ref[half % 2, at]], axis=0)
        part = f32dot(lhs, weight[...])
        total = part if total is None else total + part
    own_ref[...] = total[:rows]
    beside_ref[...] = total[rows:]


def head_pair(ref, pair):
    at = 2 * pair * HEAD_DIM
    first, second = ref[:, at : at + HEAD_DIM], ref[:, at + HEAD_DIM : at + 2 * HEAD_DIM]
    return jnp.concatenate([first, second], axis=0)


def reach(me_ref, rows, near):
    key_pos = lax.broadcasted_iota(jnp.int32, (rows, rows), 0)
    query_pos = lax.broadcasted_iota(jnp.int32, (rows, rows), 1)
    offset = (key_pos - query_pos) * (1 - 2 * (me_ref[0] % 2))
    return jnp.concatenate([offset <= 0 if near else offset >= 0] * 2, axis=1)


def columns(group):
    keys = slice(group * HEAD_DIM, (group + 1) * HEAD_DIM)
    return keys, slice(keys.start + KV_HEADS * HEAD_DIM, keys.stop + KV_HEADS * HEAD_DIM)


def near_kernel(me_ref, q_ref, g_ref, beside_ref, own_ref, lifted_ref, weighted_ref, stats_ref):
    rows = own_ref.shape[0]
    pairs = lifted_ref.shape[0]
    scale = math.log2(math.e) / math.sqrt(HEAD_DIM)
    mask = reach(me_ref, rows, True)
    for group in range(KV_HEADS):
        key_at, value_at = columns(group)
        keys = jnp.concatenate([beside_ref[:, key_at], own_ref[:, key_at]], axis=0)
        values = jnp.concatenate([beside_ref[:, value_at], own_ref[:, value_at]], axis=0)
        for pair in range(group * pairs // KV_HEADS, (group + 1) * pairs // KV_HEADS):
            scores = f32dot(keys, head_pair(q_ref, pair), NT) * scale
            scores = jnp.concatenate([jnp.where(mask, scores[:rows], -1e30), scores[rows:]], axis=0)
            peak = jnp.max(scores, axis=0, keepdims=True)
            lifted = jnp.exp2(scores - peak)
            weighted = lifted * f32dot(values, head_pair(g_ref, pair), NT)
            lifted_ref[pair] = lifted
            weighted_ref[pair] = weighted
            stats_ref[pair, 0:1] = peak
            stats_ref[pair, 1:2] = jnp.sum(lifted, axis=0, keepdims=True)
            stats_ref[pair, 2:3] = jnp.sum(weighted, axis=0, keepdims=True)


def far_kernel(me_ref, q_ref, g_ref, across_ref, stats_ref, owed_ref, d_scores_ref, rest_ref):
    rows = across_ref.shape[0]
    pairs = stats_ref.shape[0]
    scale = 1.0 / math.sqrt(HEAD_DIM)
    mask = reach(me_ref, rows, False)
    for group in range(KV_HEADS):
        key_at, value_at = columns(group)
        keys, values = across_ref[:, key_at], across_ref[:, value_at]
        d_keys = d_values = None
        for pair in range(group * pairs // KV_HEADS, (group + 1) * pairs // KV_HEADS):
            q, g = head_pair(q_ref, pair), head_pair(g_ref, pair)
            scores = f32dot(keys, q, NT) * (scale * math.log2(math.e))
            scores = jnp.where(mask, scores, -1e30)
            near_peak = stats_ref[pair, 0:1]
            peak = jnp.maximum(near_peak, jnp.max(scores, axis=0, keepdims=True))
            lifted = jnp.exp2(scores - peak)
            shrink = jnp.exp2(near_peak - peak)
            weighted = lifted * f32dot(values, g, NT)
            total = stats_ref[pair, 1:2] * shrink + jnp.sum(lifted, axis=0, keepdims=True)
            inverse = 1.0 / total
            row_dot = stats_ref[pair, 2:3] * shrink + jnp.sum(weighted, axis=0, keepdims=True)
            row_dot = row_dot * inverse
            d_scores = ((weighted - lifted * row_dot) * (inverse * scale)).astype(jnp.bfloat16)
            probs = (lifted * inverse).astype(jnp.bfloat16)
            dk, dv = f32dot(d_scores, q), f32dot(probs, g)
            d_keys = dk if d_keys is None else d_keys + dk
            d_values = dv if d_values is None else d_values + dv
            d_scores_ref[pair] = d_scores
            rest_ref[pair, 0:1] = shrink * inverse
            rest_ref[pair, 1:2] = row_dot
        owed_ref[:, key_at] = d_keys.astype(jnp.bfloat16)
        owed_ref[:, value_at] = d_values.astype(jnp.bfloat16)


def close_kernel(q_ref, g_ref, beside_ref, own_ref, across_ref, lifted_ref, weighted_ref, rest_ref, far_ref, dq_ref, db_ref, do_ref):
    rows = own_ref.shape[0]
    pairs = lifted_ref.shape[0]
    scale = 1.0 / math.sqrt(HEAD_DIM)
    for group in range(KV_HEADS):
        key_at, value_at = columns(group)
        keys = jnp.concatenate([r[:, key_at] for r in (beside_ref, own_ref, across_ref)], axis=0).T
        d_keys = d_values = None
        for pair in range(group * pairs // KV_HEADS, (group + 1) * pairs // KV_HEADS):
            lifted = lifted_ref[pair]
            part = rest_ref[pair, 0:1]
            d_scores = (weighted_ref[pair] - lifted * rest_ref[pair, 1:2]) * (part * scale)
            d_scores = d_scores.astype(jnp.bfloat16)
            probs = (lifted * part).astype(jnp.bfloat16)
            dk = f32dot(d_scores, head_pair(q_ref, pair))
            dv = f32dot(probs, head_pair(g_ref, pair))
            d_keys = dk if d_keys is None else d_keys + dk
            d_values = dv if d_values is None else d_values + dv
            dq = f32dot(keys, jnp.concatenate([d_scores, far_ref[pair]], axis=0)).astype(jnp.bfloat16)
            at = 2 * pair * HEAD_DIM
            dq_ref[:, at : at + HEAD_DIM] = dq[:, :rows].T
            dq_ref[:, at + HEAD_DIM : at + 2 * HEAD_DIM] = dq[:, rows:].T
        for at, grad in ((key_at, d_keys), (value_at, d_values)):
            db_ref[:, at] = grad[:rows].astype(jnp.bfloat16)
            do_ref[:, at] = grad[rows:]


def terms_kernel(me_ref, lent_ref, *refs):
    turned, grads, outs = refs[:3], refs[3:7], refs[7:]
    own = me_ref[0] // 4
    d_kv = jnp.concatenate([r[...] for r in grads], axis=0)
    for delta, out_ref in enumerate(outs):
        at = own ^ delta
        lhs = jnp.concatenate([turned[0][at], lent_ref[0, at].T, turned[1][at], turned[2][at]], axis=1)
        out_ref[...] = f32dot(lhs, d_kv).astype(out_ref.dtype)


def input_kernel(own_ref, beside_ref, *refs):
    weights, near_ref, lent_ref = refs[:-2], refs[-2], refs[-1]
    rows, width = own_ref.shape[0], weights[0].shape[0]
    both = jnp.concatenate([own_ref[...], beside_ref[...]], axis=0)
    for half, weight in enumerate(weights):
        part = f32dot(both, weight[...], NT)
        near_ref[half] = part[:rows]
        lent_ref[half] = part[rows:].astype(jnp.bfloat16)


def close_input_kernel(me_ref, saved_ref, factor_ref, up_ref, near_ref, lent_ref, out_ref, held):
    blocks, rows, width = held.shape
    for half in range(blocks // 2):
        delta = half // 2 * 4 + half % 2 * 2
        held[me_ref[0] ^ delta] = near_ref[half]
        held[me_ref[0] ^ delta ^ 1] = lent_ref[half].astype(jnp.float32)
    factor = factor_ref[...]
    acc = jnp.zeros((rows, width), jnp.float32)
    for b in range(blocks):
        normed = saved_ref[:, b * width : (b + 1) * width].astype(jnp.float32) * factor
        acc = acc + held[b] * normed
    mean = jnp.sum(acc, axis=-1, keepdims=True) * (1.0 / (blocks * width))
    for b in range(blocks):
        at = slice(b * width, (b + 1) * width)
        normed = saved_ref[:, at].astype(jnp.float32) * factor
        grad = up_ref[:, at].astype(jnp.float32) + factor * (held[b] - normed * mean)
        out_ref[:, at] = grad.astype(jnp.bfloat16)


def swap(block, distance):
    count = lax.axis_size("ctx")
    return lax.ppermute(block, "ctx", [(i, i ^ distance) for i in range(count)])


def shifted(block, axis, distance):
    count = lax.axis_size(axis)
    return lax.ppermute(block, axis, [((i - distance) % count, i) for i in range(count)])


def crossed(block):
    count = lax.axis_size("ctx")
    route = [(i, (i + 1) % count if i % 2 else (i - 1) % count) for i in range(count)]
    return lax.ppermute(block, "ctx", route)


def gathered(block, pieces):
    count = lax.axis_size("ctx")
    first = count // 2
    parts = {0: block, first: swap(block, first)}
    parts[2] = swap(block, 2)
    far = [0, first]
    step = first // 2
    while step >= 4:
        for d in list(far):
            parts[d ^ step] = swap(parts[d], step)
            far.append(d ^ step)
        step //= 2
    parts[4], pieces = lax.optimization_barrier((parts[4], pieces))
    parts[first], parts[2] = lax.optimization_barrier((parts[first], parts[2]))
    for d in far[1:]:
        direct = d & (first | 4) == first | 4 and first > 4
        parts[d ^ 2] = swap(parts[d ^ 4], 6) if direct else swap(parts[d], 2)
    return [parts[d] for d in range(0, count, 2)], pieces


def per_device(saved_in, grad_in, queries, d_heads, kv_weights):
    count = lax.axis_size("ctx")
    me = lax.axis_index("ctx").astype(jnp.int32).reshape(1)
    bf16, f32 = jnp.bfloat16, jnp.float32
    saved = saved_in[0]
    rows, model = saved.shape
    width, kv2 = kv_weights.shape[1:]
    tall = count // 4
    pieces = call(
        norm_kernel,
        [((2, tall, rows, width), bf16)] * 2 + [((tall, width, rows), bf16)] * 3 + [((rows, 1), f32), ((width, kv2), bf16)],
        [me, saved, kv_weights[0]],
        [pltpu.VMEM((count, rows, width), bf16), pltpu.VMEM((count, width, rows), bf16)],
    )
    weights, pieces = gathered(kv_weights[0], pieces)
    near, lent, *turned, factor, weights[0] = pieces
    lent = swap(lent, 1)
    weights[3], grad_in = lax.optimization_barrier((weights[3], grad_in))
    upstream = shifted(grad_in, "pipe", -1)[0]
    partial = ((rows, kv2), f32)
    half = ((rows, kv2), bf16)
    kv, kv_lent = call(kv_kernel, [partial, partial], [me, near, lent, *weights])
    kv = (kv + swap(kv_lent, 1)).astype(bf16)
    across = crossed(kv)
    beside = swap(kv, 1)
    pairs = model // (2 * HEAD_DIM)
    block = ((pairs, 2 * rows, 2 * rows), f32)
    lifted, weighted, stats = call(
        near_kernel,
        [block, block, ((pairs, 3, 2 * rows), f32)],
        [me, queries[0], d_heads[0], beside, kv],
    )
    stats, turned = lax.optimization_barrier((stats, turned))
    turned = [turned[0], swap(turned[1], 2), swap(turned[2], 3)]
    d_across, far, kept = call(
        far_kernel,
        [half, ((pairs, rows, 2 * rows), bf16), ((pairs, 2, 2 * rows), f32)],
        [me, queries[0], d_heads[0], across, stats],
    )
    from_across = crossed(d_across)
    d_queries, d_beside, d_own = call(
        close_kernel,
        [((rows, model), bf16), half, partial],
        [queries[0], d_heads[0], beside, kv, across, lifted, weighted, kept, far],
    )
    d_beside, turned, upstream = lax.optimization_barrier((d_beside, turned, upstream))
    from_beside = swap(d_beside, 1)
    d_kv = (d_own + from_beside.astype(f32) + from_across.astype(f32)).astype(bf16)
    above = swap(d_kv, 2)
    d_beside = swap(d_kv, 1)
    grads = [d_kv, d_beside, above, swap(above, 1)]
    terms = call(
        terms_kernel,
        [((width, kv2), f32)] + [((width, kv2), bf16)] * (tall - 1),
        [me, lent, *turned, *grads],
    )
    order = [*range(tall // 2, tall), *range(1, tall // 2)]
    received = [swap(terms[delta], 4 * delta) for delta in order]
    near, lent = call(
        input_kernel,
        [((count // 2, rows, width), f32), ((count // 2, rows, width), bf16)],
        [d_kv, d_beside, *weights],
    )
    (grad_out,) = call(
        close_input_kernel,
        [((rows, model), bf16)],
        [me, saved, factor, upstream, near, swap(lent, 1)],
        [pltpu.VMEM((count, rows, width), f32)],
    )
    received, grad_out = lax.optimization_barrier((received, grad_out))
    total = terms[0]
    for part in received:
        total = total + part.astype(f32)
    weight_grad = total * (1.0 / math.sqrt(rows * count))
    return (grad_out[None], d_queries[None], weight_grad[None])


def solution(mesh):
    spec = P("pipe", "ctx", None)
    return jax.shard_map(
        per_device, mesh=mesh, in_specs=(spec,) * 5, out_specs=(spec,) * 3, check_vma=False
    )
```

```python
import functools
import math

import jax
import jax.numpy as jnp
from jax import lax
from jax.experimental import pallas as pl
from jax.experimental.pallas import tpu as pltpu
from jax.sharding import PartitionSpec as P

HEAD_DIM = 128
KV_HEADS = 2
EPSILON = 1e-06
NT = (((1,), (1,)), ((), ()))
VMEM = pl.BlockSpec(memory_space=pltpu.VMEM)
SMEM = pl.BlockSpec(memory_space=pltpu.SMEM)
PARAMS = pltpu.CompilerParams(vmem_limit_bytes=16 * 1024 * 1024)


def f32dot(a, b, dims=(((1,), (0,)), ((), ()))):
    return lax.dot_general(a, b, dims, preferred_element_type=jnp.float32)


def call(kernel, outs, args, scratch=()):
    in_specs = [SMEM if a.dtype == jnp.int32 else VMEM for a in args]
    return pl.pallas_call(
        kernel,
        out_shape=[jax.ShapeDtypeStruct(s, d) for s, d in outs],
        in_specs=in_specs,
        out_specs=[VMEM] * len(outs),
        scratch_shapes=list(scratch),
        compiler_params=PARAMS,
    )(*args)


def norm_kernel(me_ref, saved_ref, shard_ref, near_ref, lent_ref, t0_ref, t2_ref, t3_ref, factor_ref, copy_ref, held, held_t):
    copy_ref[...] = shard_ref[...]
    blocks, _, width = held.shape
    rest = me_ref[0] % 4
    wide = saved_ref[...].astype(jnp.float32)
    factor = lax.rsqrt(jnp.mean(wide * wide, axis=-1, keepdims=True) + EPSILON)
    factor_ref[...] = factor
    normed = (wide * factor).astype(jnp.bfloat16)
    for b in range(blocks):
        part = normed[:, b * width : (b + 1) * width]
        held[b] = part
        held_t[b] = part.T
    for zz in range(blocks // 4):
        for k in range(2):
            near_ref[k, zz] = held[zz * 4 + (rest ^ (2 * k))]
            lent_ref[k, zz] = held[zz * 4 + (rest ^ (2 * k + 1))]
        for d, ref in ((0, t0_ref), (2, t2_ref), (3, t3_ref)):
            ref[zz] = held_t[zz * 4 + (rest ^ d)]


def kv_kernel(me_ref, near_ref, lent_ref, *refs):
    weights, own_ref, beside_ref = refs[:-2], refs[-2], refs[-1]
    own = me_ref[0] // 4
    rows = own_ref.shape[0]
    total = None
    for half, weight in enumerate(weights):
        at = own ^ (half // 2)
        lhs = jnp.concatenate([near_ref[half % 2, at], lent_ref[half % 2, at]], axis=0)
        part = f32dot(lhs, weight[...])
        total = part if total is None else total + part
    own_ref[...] = total[:rows]
    beside_ref[...] = total[rows:]


def head_pair(ref, pair):
    at = 2 * pair * HEAD_DIM
    first, second = ref[:, at : at + HEAD_DIM], ref[:, at + HEAD_DIM : at + 2 * HEAD_DIM]
    return jnp.concatenate([first, second], axis=0)


def reach(me_ref, rows, near):
    key_pos = lax.broadcasted_iota(jnp.int32, (rows, rows), 0)
    query_pos = lax.broadcasted_iota(jnp.int32, (rows, rows), 1)
    offset = (key_pos - query_pos) * (1 - 2 * (me_ref[0] % 2))
    return jnp.concatenate([offset <= 0 if near else offset >= 0] * 2, axis=1)


def columns(group):
    keys = slice(group * HEAD_DIM, (group + 1) * HEAD_DIM)
    return keys, slice(keys.start + KV_HEADS * HEAD_DIM, keys.stop + KV_HEADS * HEAD_DIM)


def near_kernel(me_ref, q_ref, g_ref, beside_ref, own_ref, lifted_ref, weighted_ref, stats_ref):
    rows = own_ref.shape[0]
    pairs = lifted_ref.shape[0]
    scale = math.log2(math.e) / math.sqrt(HEAD_DIM)
    mask = reach(me_ref, rows, True)
    for group in range(KV_HEADS):
        key_at, value_at = columns(group)
        keys = jnp.concatenate([beside_ref[:, key_at], own_ref[:, key_at]], axis=0)
        values = jnp.concatenate([beside_ref[:, value_at], own_ref[:, value_at]], axis=0)
        for pair in range(group * pairs // KV_HEADS, (group + 1) * pairs // KV_HEADS):
            scores = f32dot(keys, head_pair(q_ref, pair), NT) * scale
            scores = jnp.concatenate([jnp.where(mask, scores[:rows], -1e30), scores[rows:]], axis=0)
            peak = jnp.max(scores, axis=0, keepdims=True)
            lifted = jnp.exp2(scores - peak)
            weighted = lifted * f32dot(values, head_pair(g_ref, pair), NT)
            lifted_ref[pair] = lifted
            weighted_ref[pair] = weighted
            stats_ref[pair, 0:1] = peak
            stats_ref[pair, 1:2] = jnp.sum(lifted, axis=0, keepdims=True)
            stats_ref[pair, 2:3] = jnp.sum(weighted, axis=0, keepdims=True)


def far_kernel(me_ref, q_ref, g_ref, across_ref, stats_ref, owed_ref, d_scores_ref, rest_ref):
    rows = across_ref.shape[0]
    pairs = stats_ref.shape[0]
    scale = 1.0 / math.sqrt(HEAD_DIM)
    mask = reach(me_ref, rows, False)
    for group in range(KV_HEADS):
        key_at, value_at = columns(group)
        keys, values = across_ref[:, key_at], across_ref[:, value_at]
        d_keys = d_values = None
        for pair in range(group * pairs // KV_HEADS, (group + 1) * pairs // KV_HEADS):
            q, g = head_pair(q_ref, pair), head_pair(g_ref, pair)
            scores = f32dot(keys, q, NT) * (scale * math.log2(math.e))
            scores = jnp.where(mask, scores, -1e30)
            near_peak = stats_ref[pair, 0:1]
            peak = jnp.maximum(near_peak, jnp.max(scores, axis=0, keepdims=True))
            lifted = jnp.exp2(scores - peak)
            shrink = jnp.exp2(near_peak - peak)
            weighted = lifted * f32dot(values, g, NT)
            total = stats_ref[pair, 1:2] * shrink + jnp.sum(lifted, axis=0, keepdims=True)
            inverse = 1.0 / total
            row_dot = stats_ref[pair, 2:3] * shrink + jnp.sum(weighted, axis=0, keepdims=True)
            row_dot = row_dot * inverse
            d_scores = ((weighted - lifted * row_dot) * (inverse * scale)).astype(jnp.bfloat16)
            probs = (lifted * inverse).astype(jnp.bfloat16)
            dk, dv = f32dot(d_scores, q), f32dot(probs, g)
            d_keys = dk if d_keys is None else d_keys + dk
            d_values = dv if d_values is None else d_values + dv
            d_scores_ref[pair] = d_scores
            rest_ref[pair, 0:1] = shrink * inverse
            rest_ref[pair, 1:2] = row_dot
        owed_ref[:, key_at] = d_keys.astype(jnp.bfloat16)
        owed_ref[:, value_at] = d_values.astype(jnp.bfloat16)


def close_kernel(q_ref, g_ref, beside_ref, own_ref, across_ref, lifted_ref, weighted_ref, rest_ref, far_ref, dq_ref, db_ref, do_ref):
    rows = own_ref.shape[0]
    pairs = lifted_ref.shape[0]
    scale = 1.0 / math.sqrt(HEAD_DIM)
    for group in range(KV_HEADS):
        key_at, value_at = columns(group)
        keys = jnp.concatenate([r[:, key_at] for r in (beside_ref, own_ref, across_ref)], axis=0).T
        d_keys = d_values = None
        for pair in range(group * pairs // KV_HEADS, (group + 1) * pairs // KV_HEADS):
            lifted = lifted_ref[pair]
            part = rest_ref[pair, 0:1]
            d_scores = (weighted_ref[pair] - lifted * rest_ref[pair, 1:2]) * (part * scale)
            d_scores = d_scores.astype(jnp.bfloat16)
            probs = (lifted * part).astype(jnp.bfloat16)
            dk = f32dot(d_scores, head_pair(q_ref, pair))
            dv = f32dot(probs, head_pair(g_ref, pair))
            d_keys = dk if d_keys is None else d_keys + dk
            d_values = dv if d_values is None else d_values + dv
            dq = f32dot(keys, jnp.concatenate([d_scores, far_ref[pair]], axis=0)).astype(jnp.bfloat16)
            at = 2 * pair * HEAD_DIM
            dq_ref[:, at : at + HEAD_DIM] = dq[:, :rows].T
            dq_ref[:, at + HEAD_DIM : at + 2 * HEAD_DIM] = dq[:, rows:].T
        for at, grad in ((key_at, d_keys), (value_at, d_values)):
            db_ref[:, at] = grad[:rows].astype(jnp.bfloat16)
            do_ref[:, at] = grad[rows:]


def terms_kernel(me_ref, lent_ref, *refs):
    turned, grads, outs = refs[:3], refs[3:7], refs[7:]
    own = me_ref[0] // 4
    d_kv = jnp.concatenate([r[...] for r in grads], axis=0)
    for delta, out_ref in enumerate(outs):
        at = own ^ delta
        lhs = jnp.concatenate([turned[0][at], lent_ref[0, at].T, turned[1][at], turned[2][at]], axis=1)
        out_ref[...] = f32dot(lhs, d_kv).astype(out_ref.dtype)


def input_kernel(own_ref, beside_ref, *refs):
    weights, near_ref, lent_ref = refs[:-2], refs[-2], refs[-1]
    rows, width = own_ref.shape[0], weights[0].shape[0]
    both = jnp.concatenate([own_ref[...], beside_ref[...]], axis=0)
    for half, weight in enumerate(weights):
        part = f32dot(both, weight[...], NT)
        near_ref[half] = part[:rows]
        lent_ref[half] = part[rows:].astype(jnp.bfloat16)


def close_input_kernel(me_ref, saved_ref, factor_ref, up_ref, near_ref, lent_ref, out_ref, held):
    blocks, rows, width = held.shape
    for half in range(blocks // 2):
        delta = half // 2 * 4 + half % 2 * 2
        held[me_ref[0] ^ delta] = near_ref[half]
        held[me_ref[0] ^ delta ^ 1] = lent_ref[half].astype(jnp.float32)
    factor = factor_ref[...]
    acc = jnp.zeros((rows, width), jnp.float32)
    for b in range(blocks):
        normed = saved_ref[:, b * width : (b + 1) * width].astype(jnp.float32) * factor
        acc = acc + held[b] * normed
    mean = jnp.sum(acc, axis=-1, keepdims=True) * (1.0 / (blocks * width))
    for b in range(blocks):
        at = slice(b * width, (b + 1) * width)
        normed = saved_ref[:, at].astype(jnp.float32) * factor
        grad = up_ref[:, at].astype(jnp.float32) + factor * (held[b] - normed * mean)
        out_ref[:, at] = grad.astype(jnp.bfloat16)


def swap(block, distance):
    count = lax.axis_size("ctx")
    return lax.ppermute(block, "ctx", [(i, i ^ distance) for i in range(count)])


def shifted(block, axis, distance):
    count = lax.axis_size(axis)
    return lax.ppermute(block, axis, [((i - distance) % count, i) for i in range(count)])


def crossed(block):
    count = lax.axis_size("ctx")
    route = [(i, (i + 1) % count if i % 2 else (i - 1) % count) for i in range(count)]
    return lax.ppermute(block, "ctx", route)


def gathered(block, pieces):
    count = lax.axis_size("ctx")
    first = count // 2
    parts = {0: block, first: swap(block, first)}
    parts[2] = swap(block, 2)
    far = [0, first]
    step = first // 2
    while step >= 4:
        for d in list(far):
            parts[d ^ step] = swap(parts[d], step)
            far.append(d ^ step)
        step //= 2
    parts[4], pieces = lax.optimization_barrier((parts[4], pieces))
    parts[first], parts[2] = lax.optimization_barrier((parts[first], parts[2]))
    for d in far[1:]:
        direct = d & (first | 4) == first | 4 and first > 4
        parts[d ^ 2] = swap(parts[d ^ 4], 6) if direct else swap(parts[d], 2)
    return [parts[d] for d in range(0, count, 2)], pieces


def per_device(saved_in, grad_in, queries, d_heads, kv_weights):
    count = lax.axis_size("ctx")
    me = lax.axis_index("ctx").astype(jnp.int32).reshape(1)
    bf16, f32 = jnp.bfloat16, jnp.float32
    saved = saved_in[0]
    rows, model = saved.shape
    width, kv2 = kv_weights.shape[1:]
    tall = count // 4
    pieces = call(
        norm_kernel,
        [((2, tall, rows, width), bf16)] * 2 + [((tall, width, rows), bf16)] * 3 + [((rows, 1), f32), ((width, kv2), bf16)],
        [me, saved, kv_weights[0]],
        [pltpu.VMEM((count, rows, width), bf16), pltpu.VMEM((count, width, rows), bf16)],
    )
    weights, pieces = gathered(kv_weights[0], pieces)
    near, lent, *turned, factor, weights[0] = pieces
    lent = swap(lent, 1)
    weights[3], grad_in = lax.optimization_barrier((weights[3], grad_in))
    upstream = shifted(grad_in, "pipe", -1)[0]
    partial = ((rows, kv2), f32)
    half = ((rows, kv2), bf16)
    kv, kv_lent = call(kv_kernel, [partial, partial], [me, near, lent, *weights])
    kv = (kv + swap(kv_lent, 1)).astype(bf16)
    across = crossed(kv)
    beside = swap(kv, 1)
    pairs = model // (2 * HEAD_DIM)
    block = ((pairs, 2 * rows, 2 * rows), f32)
    lifted, weighted, stats = call(
        near_kernel,
        [block, block, ((pairs, 3, 2 * rows), f32)],
        [me, queries[0], d_heads[0], beside, kv],
    )
    stats, turned = lax.optimization_barrier((stats, turned))
    turned = [turned[0], swap(turned[1], 2), swap(turned[2], 3)]
    d_across, far, kept = call(
        far_kernel,
        [half, ((pairs, rows, 2 * rows), bf16), ((pairs, 2, 2 * rows), f32)],
        [me, queries[0], d_heads[0], across, stats],
    )
    from_across = crossed(d_across)
    d_queries, d_beside, d_own = call(
        close_kernel,
        [((rows, model), bf16), half, partial],
        [queries[0], d_heads[0], beside, kv, across, lifted, weighted, kept, far],
    )
    d_beside, turned, upstream = lax.optimization_barrier((d_beside, turned, upstream))
    from_beside = swap(d_beside, 1)
    d_kv = (d_own + from_beside.astype(f32) + from_across.astype(f32)).astype(bf16)
    above = swap(d_kv, 2)
    d_beside = swap(d_kv, 1)
    grads = [d_kv, d_beside, above, swap(above, 1)]
    terms = call(
        terms_kernel,
        [((width, kv2), f32)] + [((width, kv2), bf16)] * (tall - 1),
        [me, lent, *turned, *grads],
    )
    order = [tall // 2, *range(1, tall // 2), *range(tall // 2 + 1, tall)]
    received = [swap(terms[delta], 4 * delta) for delta in order]
    near, lent = call(
        input_kernel,
        [((count // 2, rows, width), f32), ((count // 2, rows, width), bf16)],
        [d_kv, d_beside, *weights],
    )
    (grad_out,) = call(
        close_input_kernel,
        [((rows, model), bf16)],
        [me, saved, factor, upstream, near, swap(lent, 1)],
        [pltpu.VMEM((count, rows, width), f32)],
    )
    received, grad_out = lax.optimization_barrier((received, grad_out))
    total = terms[0]
    for part in received:
        total = total + part.astype(f32)
    weight_grad = total * (1.0 / math.sqrt(rows * count))
    return (grad_out[None], d_queries[None], weight_grad[None])


def solution(mesh):
    spec = P("pipe", "ctx", None)
    return jax.shard_map(
        per_device, mesh=mesh, in_specs=(spec,) * 5, out_specs=(spec,) * 3, check_vma=False
    )
```

```python
import functools
import math

import jax
import jax.numpy as jnp
from jax import lax
from jax.experimental import pallas as pl
from jax.experimental.pallas import tpu as pltpu
from jax.sharding import PartitionSpec as P

HEAD_DIM = 128
BATCH = 8
KV_HEADS = 2
EPSILON = 1e-06
NT = (((1,), (1,)), ((), ()))
VMEM = pl.BlockSpec(memory_space=pltpu.VMEM)
SMEM = pl.BlockSpec(memory_space=pltpu.SMEM)
PARAMS = pltpu.CompilerParams(vmem_limit_bytes=16 * 1024 * 1024)


def f32dot(a, b, dims=(((1,), (0,)), ((), ()))):
    return lax.dot_general(a, b, dims, preferred_element_type=jnp.float32)


def call(kernel, outs, args, scratch=()):
    in_specs = [SMEM if a.dtype == jnp.int32 else VMEM for a in args]
    return pl.pallas_call(
        kernel,
        out_shape=[jax.ShapeDtypeStruct(s, d) for s, d in outs],
        in_specs=in_specs,
        out_specs=[VMEM] * len(outs),
        scratch_shapes=list(scratch),
        compiler_params=PARAMS,
    )(*args)


def norm_kernel(me_ref, saved_ref, shard_ref, near_ref, lent_ref, t0_ref, t2_ref, t3_ref, factor_ref, copy_ref, held, held_t):
    copy_ref[...] = shard_ref[...]
    blocks, _, width = held.shape
    rest = me_ref[0] % 4
    wide = saved_ref[...].astype(jnp.float32)
    factor = lax.rsqrt(jnp.mean(wide * wide, axis=-1, keepdims=True) + EPSILON)
    factor_ref[...] = factor
    normed = (wide * factor).astype(jnp.bfloat16)
    for b in range(blocks):
        part = normed[:, b * width : (b + 1) * width]
        held[b] = part
        held_t[b] = part.T
    for zz in range(blocks // 4):
        for k in range(2):
            near_ref[k, zz] = held[zz * 4 + (rest ^ (2 * k))]
            lent_ref[k, zz] = held[zz * 4 + (rest ^ (2 * k + 1))]
        for d, ref in ((0, t0_ref), (2, t2_ref), (3, t3_ref)):
            ref[zz] = held_t[zz * 4 + (rest ^ d)]


def kv_kernel(me_ref, near_ref, lent_ref, *refs):
    weights, own_ref, beside_ref = refs[:-2], refs[-2], refs[-1]
    own = me_ref[0] // 4
    rows = own_ref.shape[0]
    total = None
    for half, weight in enumerate(weights):
        at = own ^ (half // 2)
        lhs = jnp.concatenate([near_ref[half % 2, at], lent_ref[half % 2, at]], axis=0)
        part = f32dot(lhs, weight[...])
        total = part if total is None else total + part
    own_ref[...] = total[:rows]
    beside_ref[...] = total[rows:]


def head_rows(ref, block, size):
    at = block * size * HEAD_DIM
    return jnp.concatenate([ref[:, at + h * HEAD_DIM : at + (h + 1) * HEAD_DIM] for h in range(size)], axis=0)


def reach(me_ref, rows, near):
    key_pos = lax.broadcasted_iota(jnp.int32, (rows, rows), 0)
    query_pos = lax.broadcasted_iota(jnp.int32, (rows, rows), 1)
    offset = (key_pos - query_pos) * (1 - 2 * (me_ref[0] % 2))
    return jnp.concatenate([offset <= 0 if near else offset >= 0] * BATCH, axis=1)


def columns(group):
    keys = slice(group * HEAD_DIM, (group + 1) * HEAD_DIM)
    return keys, slice(keys.start + KV_HEADS * HEAD_DIM, keys.stop + KV_HEADS * HEAD_DIM)


def near_kernel(me_ref, q_ref, g_ref, beside_ref, own_ref, lifted_ref, weighted_ref, stats_ref):
    rows = own_ref.shape[0]
    pairs = lifted_ref.shape[0]
    scale = math.log2(math.e) / math.sqrt(HEAD_DIM)
    mask = reach(me_ref, rows, True)
    for group in range(KV_HEADS):
        key_at, value_at = columns(group)
        keys = jnp.concatenate([beside_ref[:, key_at], own_ref[:, key_at]], axis=0)
        values = jnp.concatenate([beside_ref[:, value_at], own_ref[:, value_at]], axis=0)
        for pair in range(group * pairs // KV_HEADS, (group + 1) * pairs // KV_HEADS):
            scores = f32dot(keys, head_rows(q_ref, pair, BATCH), NT) * scale
            scores = jnp.concatenate([jnp.where(mask, scores[:rows], -1e30), scores[rows:]], axis=0)
            peak = jnp.max(scores, axis=0, keepdims=True)
            lifted = jnp.exp2(scores - peak)
            weighted = lifted * f32dot(values, head_rows(g_ref, pair, BATCH), NT)
            lifted_ref[pair] = lifted
            weighted_ref[pair] = weighted
            stats_ref[pair, 0:1] = peak
            stats_ref[pair, 1:2] = jnp.sum(lifted, axis=0, keepdims=True)
            stats_ref[pair, 2:3] = jnp.sum(weighted, axis=0, keepdims=True)


def far_kernel(me_ref, q_ref, g_ref, across_ref, stats_ref, owed_ref, d_scores_ref, rest_ref):
    rows = across_ref.shape[0]
    pairs = stats_ref.shape[0]
    scale = 1.0 / math.sqrt(HEAD_DIM)
    mask = reach(me_ref, rows, False)
    for group in range(KV_HEADS):
        key_at, value_at = columns(group)
        keys, values = across_ref[:, key_at], across_ref[:, value_at]
        d_keys = d_values = None
        for pair in range(group * pairs // KV_HEADS, (group + 1) * pairs // KV_HEADS):
            q, g = head_rows(q_ref, pair, BATCH), head_rows(g_ref, pair, BATCH)
            scores = f32dot(keys, q, NT) * (scale * math.log2(math.e))
            scores = jnp.where(mask, scores, -1e30)
            near_peak = stats_ref[pair, 0:1]
            peak = jnp.maximum(near_peak, jnp.max(scores, axis=0, keepdims=True))
            lifted = jnp.exp2(scores - peak)
            shrink = jnp.exp2(near_peak - peak)
            weighted = lifted * f32dot(values, g, NT)
            total = stats_ref[pair, 1:2] * shrink + jnp.sum(lifted, axis=0, keepdims=True)
            inverse = 1.0 / total
            row_dot = stats_ref[pair, 2:3] * shrink + jnp.sum(weighted, axis=0, keepdims=True)
            row_dot = row_dot * inverse
            d_scores = ((weighted - lifted * row_dot) * (inverse * scale)).astype(jnp.bfloat16)
            probs = (lifted * inverse).astype(jnp.bfloat16)
            dk, dv = f32dot(d_scores, q), f32dot(probs, g)
            d_keys = dk if d_keys is None else d_keys + dk
            d_values = dv if d_values is None else d_values + dv
            d_scores_ref[pair] = d_scores
            rest_ref[pair, 0:1] = shrink * inverse
            rest_ref[pair, 1:2] = row_dot
        owed_ref[:, key_at] = d_keys.astype(jnp.bfloat16)
        owed_ref[:, value_at] = d_values.astype(jnp.bfloat16)


def close_kernel(q_ref, g_ref, beside_ref, own_ref, across_ref, lifted_ref, weighted_ref, rest_ref, far_ref, dq_ref, db_ref, do_ref):
    rows = own_ref.shape[0]
    pairs = lifted_ref.shape[0]
    scale = 1.0 / math.sqrt(HEAD_DIM)
    for group in range(KV_HEADS):
        key_at, value_at = columns(group)
        keys = jnp.concatenate([r[:, key_at] for r in (beside_ref, own_ref, across_ref)], axis=0).T
        d_keys = d_values = None
        for pair in range(group * pairs // KV_HEADS, (group + 1) * pairs // KV_HEADS):
            lifted = lifted_ref[pair]
            part = rest_ref[pair, 0:1]
            d_scores = (weighted_ref[pair] - lifted * rest_ref[pair, 1:2]) * (part * scale)
            d_scores = d_scores.astype(jnp.bfloat16)
            probs = (lifted * part).astype(jnp.bfloat16)
            dk = f32dot(d_scores, head_rows(q_ref, pair, BATCH))
            dv = f32dot(probs, head_rows(g_ref, pair, BATCH))
            d_keys = dk if d_keys is None else d_keys + dk
            d_values = dv if d_values is None else d_values + dv
            dq = f32dot(keys, jnp.concatenate([d_scores, far_ref[pair]], axis=0)).astype(jnp.bfloat16)
            for h in range(BATCH):
                at = (BATCH * pair + h) * HEAD_DIM
                dq_ref[:, at : at + HEAD_DIM] = dq[:, h * rows : (h + 1) * rows].T
        for at, grad in ((key_at, d_keys), (value_at, d_values)):
            db_ref[:, at] = grad[:rows].astype(jnp.bfloat16)
            do_ref[:, at] = grad[rows:]


def terms_kernel(me_ref, lent_ref, *refs):
    turned, grads, outs = refs[:3], refs[3:7], refs[7:]
    own = me_ref[0] // 4
    d_kv = jnp.concatenate([r[...] for r in grads], axis=0)
    for delta, out_ref in enumerate(outs):
        at = own ^ delta
        lhs = jnp.concatenate([turned[0][at], lent_ref[0, at].T, turned[1][at], turned[2][at]], axis=1)
        out_ref[...] = f32dot(lhs, d_kv).astype(out_ref.dtype)


def input_kernel(own_ref, beside_ref, *refs):
    weights, near_ref, lent_ref = refs[:-2], refs[-2], refs[-1]
    rows, width = own_ref.shape[0], weights[0].shape[0]
    both = jnp.concatenate([own_ref[...], beside_ref[...]], axis=0)
    for half, weight in enumerate(weights):
        part = f32dot(both, weight[...], NT)
        near_ref[half] = part[:rows]
        lent_ref[half] = part[rows:].astype(jnp.bfloat16)


def close_input_kernel(me_ref, saved_ref, factor_ref, up_ref, near_ref, lent_ref, out_ref, held):
    blocks, rows, width = held.shape
    for half in range(blocks // 2):
        delta = half // 2 * 4 + half % 2 * 2
        held[me_ref[0] ^ delta] = near_ref[half]
        held[me_ref[0] ^ delta ^ 1] = lent_ref[half].astype(jnp.float32)
    factor = factor_ref[...]
    acc = jnp.zeros((rows, width), jnp.float32)
    for b in range(blocks):
        normed = saved_ref[:, b * width : (b + 1) * width].astype(jnp.float32) * factor
        acc = acc + held[b] * normed
    mean = jnp.sum(acc, axis=-1, keepdims=True) * (1.0 / (blocks * width))
    for b in range(blocks):
        at = slice(b * width, (b + 1) * width)
        normed = saved_ref[:, at].astype(jnp.float32) * factor
        grad = up_ref[:, at].astype(jnp.float32) + factor * (held[b] - normed * mean)
        out_ref[:, at] = grad.astype(jnp.bfloat16)


def swap(block, distance):
    count = lax.axis_size("ctx")
    return lax.ppermute(block, "ctx", [(i, i ^ distance) for i in range(count)])


def shifted(block, axis, distance):
    count = lax.axis_size(axis)
    return lax.ppermute(block, axis, [((i - distance) % count, i) for i in range(count)])


def crossed(block):
    count = lax.axis_size("ctx")
    route = [(i, (i + 1) % count if i % 2 else (i - 1) % count) for i in range(count)]
    return lax.ppermute(block, "ctx", route)


def gathered(block, pieces):
    count = lax.axis_size("ctx")
    first = count // 2
    parts = {0: block, first: swap(block, first)}
    parts[2] = swap(block, 2)
    far = [0, first]
    step = first // 2
    while step >= 4:
        for d in list(far):
            parts[d ^ step] = swap(parts[d], step)
            far.append(d ^ step)
        step //= 2
    parts[4], pieces = lax.optimization_barrier((parts[4], pieces))
    parts[first], parts[2] = lax.optimization_barrier((parts[first], parts[2]))
    for d in far[1:]:
        direct = d & (first | 4) == first | 4 and first > 4
        parts[d ^ 2] = swap(parts[d ^ 4], 6) if direct else swap(parts[d], 2)
    return [parts[d] for d in range(0, count, 2)], pieces


def per_device(saved_in, grad_in, queries, d_heads, kv_weights):
    count = lax.axis_size("ctx")
    me = lax.axis_index("ctx").astype(jnp.int32).reshape(1)
    bf16, f32 = jnp.bfloat16, jnp.float32
    saved = saved_in[0]
    rows, model = saved.shape
    width, kv2 = kv_weights.shape[1:]
    tall = count // 4
    pieces = call(
        norm_kernel,
        [((2, tall, rows, width), bf16)] * 2 + [((tall, width, rows), bf16)] * 3 + [((rows, 1), f32), ((width, kv2), bf16)],
        [me, saved, kv_weights[0]],
        [pltpu.VMEM((count, rows, width), bf16), pltpu.VMEM((count, width, rows), bf16)],
    )
    weights, pieces = gathered(kv_weights[0], pieces)
    near, lent, *turned, factor, weights[0] = pieces
    lent = swap(lent, 1)
    weights[3], grad_in = lax.optimization_barrier((weights[3], grad_in))
    upstream = shifted(grad_in, "pipe", -1)[0]
    partial = ((rows, kv2), f32)
    half = ((rows, kv2), bf16)
    kv, kv_lent = call(kv_kernel, [partial, partial], [me, near, lent, *weights])
    kv = (kv + swap(kv_lent, 1)).astype(bf16)
    across = crossed(kv)
    beside = swap(kv, 1)
    pairs = model // (BATCH * HEAD_DIM)
    block = ((pairs, 2 * rows, BATCH * rows), f32)
    lifted, weighted, stats = call(
        near_kernel,
        [block, block, ((pairs, 3, BATCH * rows), f32)],
        [me, queries[0], d_heads[0], beside, kv],
    )
    stats, turned = lax.optimization_barrier((stats, turned))
    turned = [turned[0], swap(turned[1], 2), swap(turned[2], 3)]
    d_across, far, kept = call(
        far_kernel,
        [half, ((pairs, rows, BATCH * rows), bf16), ((pairs, 2, BATCH * rows), f32)],
        [me, queries[0], d_heads[0], across, stats],
    )
    from_across = crossed(d_across)
    d_queries, d_beside, d_own = call(
        close_kernel,
        [((rows, model), bf16), half, partial],
        [queries[0], d_heads[0], beside, kv, across, lifted, weighted, kept, far],
    )
    d_beside, turned, upstream = lax.optimization_barrier((d_beside, turned, upstream))
    from_beside = swap(d_beside, 1)
    d_kv = (d_own + from_beside.astype(f32) + from_across.astype(f32)).astype(bf16)
    above = swap(d_kv, 2)
    d_beside = swap(d_kv, 1)
    grads = [d_kv, d_beside, above, swap(above, 1)]
    terms = call(
        terms_kernel,
        [((width, kv2), f32)] + [((width, kv2), bf16)] * (tall - 1),
        [me, lent, *turned, *grads],
    )
    order = [tall // 2, *range(1, tall // 2), *range(tall // 2 + 1, tall)]
    received = [swap(terms[delta], 4 * delta) for delta in order]
    near, lent = call(
        input_kernel,
        [((count // 2, rows, width), f32), ((count // 2, rows, width), bf16)],
        [d_kv, d_beside, *weights],
    )
    (grad_out,) = call(
        close_input_kernel,
        [((rows, model), bf16)],
        [me, saved, factor, upstream, near, swap(lent, 1)],
        [pltpu.VMEM((count, rows, width), f32)],
    )
    received, grad_out = lax.optimization_barrier((received, grad_out))
    total = terms[0]
    for part in received:
        total = total + part.astype(f32)
    weight_grad = total * (1.0 / math.sqrt(rows * count))
    return (grad_out[None], d_queries[None], weight_grad[None])


def solution(mesh):
    spec = P("pipe", "ctx", None)
    return jax.shard_map(
        per_device, mesh=mesh, in_specs=(spec,) * 5, out_specs=(spec,) * 3, check_vma=False
    )
```

```python
import functools
import math

import jax
import jax.numpy as jnp
from jax import lax
from jax.experimental import pallas as pl
from jax.experimental.pallas import tpu as pltpu
from jax.sharding import PartitionSpec as P

HEAD_DIM = 128
BATCH = 8
KV_HEADS = 2
EPSILON = 1e-06
NT = (((1,), (1,)), ((), ()))
VMEM = pl.BlockSpec(memory_space=pltpu.VMEM)
SMEM = pl.BlockSpec(memory_space=pltpu.SMEM)
PARAMS = pltpu.CompilerParams(vmem_limit_bytes=16 * 1024 * 1024)


def f32dot(a, b, dims=(((1,), (0,)), ((), ()))):
    return lax.dot_general(a, b, dims, preferred_element_type=jnp.float32)


def call(kernel, outs, args, scratch=()):
    in_specs = [SMEM if a.dtype == jnp.int32 else VMEM for a in args]
    return pl.pallas_call(
        kernel,
        out_shape=[jax.ShapeDtypeStruct(s, d) for s, d in outs],
        in_specs=in_specs,
        out_specs=[VMEM] * len(outs),
        scratch_shapes=list(scratch),
        compiler_params=PARAMS,
    )(*args)


def norm_kernel(me_ref, saved_ref, shard_ref, near_ref, lent_ref, t0_ref, t2_ref, t3_ref, factor_ref, copy_ref, held, held_t):
    copy_ref[...] = shard_ref[...]
    blocks, _, width = held.shape
    rest = me_ref[0] % 4
    wide = saved_ref[...].astype(jnp.float32)
    factor = lax.rsqrt(jnp.mean(wide * wide, axis=-1, keepdims=True) + EPSILON)
    factor_ref[...] = factor
    normed = (wide * factor).astype(jnp.bfloat16)
    for b in range(blocks):
        part = normed[:, b * width : (b + 1) * width]
        held[b] = part
        held_t[b] = part.T
    for zz in range(blocks // 4):
        for k in range(2):
            near_ref[k, zz] = held[zz * 4 + (rest ^ (2 * k))]
            lent_ref[k, zz] = held[zz * 4 + (rest ^ (2 * k + 1))]
        for d, ref in ((0, t0_ref), (2, t2_ref), (3, t3_ref)):
            ref[zz] = held_t[zz * 4 + (rest ^ d)]


def kv_kernel(me_ref, near_ref, lent_ref, *refs):
    weights, own_ref, beside_ref = refs[:-2], refs[-2], refs[-1]
    own = me_ref[0] // 4
    rows = own_ref.shape[0]
    total = None
    for zz in range(len(weights) // 2):
        at = own ^ zz
        lhs = [jnp.concatenate([near_ref[k, at], lent_ref[k, at]], axis=0) for k in range(2)]
        rhs = jnp.concatenate([weights[2 * zz][...], weights[2 * zz + 1][...]], axis=0)
        part = f32dot(jnp.concatenate(lhs, axis=1), rhs)
        total = part if total is None else total + part
    own_ref[...] = total[:rows]
    beside_ref[...] = total[rows:]


def head_rows(ref, block, size):
    at = block * size * HEAD_DIM
    return jnp.concatenate([ref[:, at + h * HEAD_DIM : at + (h + 1) * HEAD_DIM] for h in range(size)], axis=0)


def reach(me_ref, rows, near):
    key_pos = lax.broadcasted_iota(jnp.int32, (rows, rows), 0)
    query_pos = lax.broadcasted_iota(jnp.int32, (rows, rows), 1)
    offset = (key_pos - query_pos) * (1 - 2 * (me_ref[0] % 2))
    return jnp.concatenate([offset <= 0 if near else offset >= 0] * BATCH, axis=1)


def columns(group):
    keys = slice(group * HEAD_DIM, (group + 1) * HEAD_DIM)
    return keys, slice(keys.start + KV_HEADS * HEAD_DIM, keys.stop + KV_HEADS * HEAD_DIM)


def near_kernel(me_ref, q_ref, g_ref, beside_ref, own_ref, lifted_ref, weighted_ref, stats_ref):
    rows = own_ref.shape[0]
    pairs = lifted_ref.shape[0]
    scale = math.log2(math.e) / math.sqrt(HEAD_DIM)
    mask = reach(me_ref, rows, True)
    for group in range(KV_HEADS):
        key_at, value_at = columns(group)
        keys = jnp.concatenate([beside_ref[:, key_at], own_ref[:, key_at]], axis=0)
        values = jnp.concatenate([beside_ref[:, value_at], own_ref[:, value_at]], axis=0)
        for pair in range(group * pairs // KV_HEADS, (group + 1) * pairs // KV_HEADS):
            scores = f32dot(keys, head_rows(q_ref, pair, BATCH), NT) * scale
            scores = jnp.concatenate([jnp.where(mask, scores[:rows], -1e30), scores[rows:]], axis=0)
            peak = jnp.max(scores, axis=0, keepdims=True)
            lifted = jnp.exp2(scores - peak)
            weighted = lifted * f32dot(values, head_rows(g_ref, pair, BATCH), NT)
            lifted_ref[pair] = lifted
            weighted_ref[pair] = weighted
            stats_ref[pair, 0:1] = peak
            stats_ref[pair, 1:2] = jnp.sum(lifted, axis=0, keepdims=True)
            stats_ref[pair, 2:3] = jnp.sum(weighted, axis=0, keepdims=True)


def far_kernel(me_ref, q_ref, g_ref, across_ref, stats_ref, owed_ref, d_scores_ref, rest_ref):
    rows = across_ref.shape[0]
    pairs = stats_ref.shape[0]
    scale = 1.0 / math.sqrt(HEAD_DIM)
    mask = reach(me_ref, rows, False)
    for group in range(KV_HEADS):
        key_at, value_at = columns(group)
        keys, values = across_ref[:, key_at], across_ref[:, value_at]
        d_keys = d_values = None
        for pair in range(group * pairs // KV_HEADS, (group + 1) * pairs // KV_HEADS):
            q, g = head_rows(q_ref, pair, BATCH), head_rows(g_ref, pair, BATCH)
            scores = f32dot(keys, q, NT) * (scale * math.log2(math.e))
            scores = jnp.where(mask, scores, -1e30)
            near_peak = stats_ref[pair, 0:1]
            peak = jnp.maximum(near_peak, jnp.max(scores, axis=0, keepdims=True))
            lifted = jnp.exp2(scores - peak)
            shrink = jnp.exp2(near_peak - peak)
            weighted = lifted * f32dot(values, g, NT)
            total = stats_ref[pair, 1:2] * shrink + jnp.sum(lifted, axis=0, keepdims=True)
            inverse = 1.0 / total
            row_dot = stats_ref[pair, 2:3] * shrink + jnp.sum(weighted, axis=0, keepdims=True)
            row_dot = row_dot * inverse
            d_scores = ((weighted - lifted * row_dot) * (inverse * scale)).astype(jnp.bfloat16)
            probs = (lifted * inverse).astype(jnp.bfloat16)
            dk, dv = f32dot(d_scores, q), f32dot(probs, g)
            d_keys = dk if d_keys is None else d_keys + dk
            d_values = dv if d_values is None else d_values + dv
            d_scores_ref[pair] = d_scores
            rest_ref[pair, 0:1] = shrink * inverse
            rest_ref[pair, 1:2] = row_dot
        owed_ref[:, key_at] = d_keys.astype(jnp.bfloat16)
        owed_ref[:, value_at] = d_values.astype(jnp.bfloat16)


def close_kernel(q_ref, g_ref, beside_ref, own_ref, across_ref, lifted_ref, weighted_ref, rest_ref, far_ref, dq_ref, db_ref, do_ref):
    rows = own_ref.shape[0]
    pairs = lifted_ref.shape[0]
    scale = 1.0 / math.sqrt(HEAD_DIM)
    for group in range(KV_HEADS):
        key_at, value_at = columns(group)
        keys = jnp.concatenate([r[:, key_at] for r in (beside_ref, own_ref, across_ref)], axis=0).T
        d_keys = d_values = None
        for pair in range(group * pairs // KV_HEADS, (group + 1) * pairs // KV_HEADS):
            lifted = lifted_ref[pair]
            part = rest_ref[pair, 0:1]
            d_scores = (weighted_ref[pair] - lifted * rest_ref[pair, 1:2]) * (part * scale)
            d_scores = d_scores.astype(jnp.bfloat16)
            probs = (lifted * part).astype(jnp.bfloat16)
            dk = f32dot(d_scores, head_rows(q_ref, pair, BATCH))
            dv = f32dot(probs, head_rows(g_ref, pair, BATCH))
            d_keys = dk if d_keys is None else d_keys + dk
            d_values = dv if d_values is None else d_values + dv
            dq = f32dot(keys, jnp.concatenate([d_scores, far_ref[pair]], axis=0)).astype(jnp.bfloat16)
            for h in range(BATCH):
                at = (BATCH * pair + h) * HEAD_DIM
                dq_ref[:, at : at + HEAD_DIM] = dq[:, h * rows : (h + 1) * rows].T
        for at, grad in ((key_at, d_keys), (value_at, d_values)):
            db_ref[:, at] = grad[:rows].astype(jnp.bfloat16)
            do_ref[:, at] = grad[rows:]


def terms_kernel(me_ref, lent_ref, *refs):
    turned, grads, outs = refs[:3], refs[3:7], refs[7:]
    own = me_ref[0] // 4
    d_kv = jnp.concatenate([r[...] for r in grads], axis=0)
    for delta, out_ref in enumerate(outs):
        at = own ^ delta
        lhs = jnp.concatenate([turned[0][at], lent_ref[0, at].T, turned[1][at], turned[2][at]], axis=1)
        out_ref[...] = f32dot(lhs, d_kv).astype(out_ref.dtype)


def input_kernel(own_ref, beside_ref, *refs):
    weights, near_ref, lent_ref = refs[:-2], refs[-2], refs[-1]
    rows, width = own_ref.shape[0], weights[0].shape[0]
    both = jnp.concatenate([own_ref[...], beside_ref[...]], axis=0)
    for half, weight in enumerate(weights):
        part = f32dot(both, weight[...], NT)
        near_ref[half] = part[:rows]
        lent_ref[half] = part[rows:].astype(jnp.bfloat16)


def close_input_kernel(me_ref, saved_ref, factor_ref, up_ref, near_ref, lent_ref, out_ref, held):
    blocks, rows, width = held.shape
    for half in range(blocks // 2):
        delta = half // 2 * 4 + half % 2 * 2
        held[me_ref[0] ^ delta] = near_ref[half]
        held[me_ref[0] ^ delta ^ 1] = lent_ref[half].astype(jnp.float32)
    factor = factor_ref[...]
    acc = jnp.zeros((rows, width), jnp.float32)
    for b in range(blocks):
        normed = saved_ref[:, b * width : (b + 1) * width].astype(jnp.float32) * factor
        acc = acc + held[b] * normed
    mean = jnp.sum(acc, axis=-1, keepdims=True) * (1.0 / (blocks * width))
    for b in range(blocks):
        at = slice(b * width, (b + 1) * width)
        normed = saved_ref[:, at].astype(jnp.float32) * factor
        grad = up_ref[:, at].astype(jnp.float32) + factor * (held[b] - normed * mean)
        out_ref[:, at] = grad.astype(jnp.bfloat16)


def swap(block, distance):
    count = lax.axis_size("ctx")
    return lax.ppermute(block, "ctx", [(i, i ^ distance) for i in range(count)])


def shifted(block, axis, distance):
    count = lax.axis_size(axis)
    return lax.ppermute(block, axis, [((i - distance) % count, i) for i in range(count)])


def crossed(block):
    count = lax.axis_size("ctx")
    route = [(i, (i + 1) % count if i % 2 else (i - 1) % count) for i in range(count)]
    return lax.ppermute(block, "ctx", route)


def gathered(block, pieces):
    count = lax.axis_size("ctx")
    first = count // 2
    parts = {0: block, first: swap(block, first)}
    parts[2] = swap(block, 2)
    far = [0, first]
    step = first // 2
    while step >= 4:
        for d in list(far):
            parts[d ^ step] = swap(parts[d], step)
            far.append(d ^ step)
        step //= 2
    parts[4], pieces = lax.optimization_barrier((parts[4], pieces))
    parts[first], parts[2] = lax.optimization_barrier((parts[first], parts[2]))
    for d in far[1:]:
        direct = d & (first | 4) == first | 4 and first > 4
        parts[d ^ 2] = swap(parts[d ^ 4], 6) if direct else swap(parts[d], 2)
    return [parts[d] for d in range(0, count, 2)], pieces


def per_device(saved_in, grad_in, queries, d_heads, kv_weights):
    count = lax.axis_size("ctx")
    me = lax.axis_index("ctx").astype(jnp.int32).reshape(1)
    bf16, f32 = jnp.bfloat16, jnp.float32
    saved = saved_in[0]
    rows, model = saved.shape
    width, kv2 = kv_weights.shape[1:]
    tall = count // 4
    pieces = call(
        norm_kernel,
        [((2, tall, rows, width), bf16)] * 2 + [((tall, width, rows), bf16)] * 3 + [((rows, 1), f32), ((width, kv2), bf16)],
        [me, saved, kv_weights[0]],
        [pltpu.VMEM((count, rows, width), bf16), pltpu.VMEM((count, width, rows), bf16)],
    )
    weights, pieces = gathered(kv_weights[0], pieces)
    near, lent, *turned, factor, weights[0] = pieces
    lent = swap(lent, 1)
    weights[3], grad_in = lax.optimization_barrier((weights[3], grad_in))
    upstream = shifted(grad_in, "pipe", -1)[0]
    partial = ((rows, kv2), f32)
    half = ((rows, kv2), bf16)
    kv, kv_lent = call(kv_kernel, [partial, partial], [me, near, lent, *weights])
    kv = (kv + swap(kv_lent, 1)).astype(bf16)
    across = crossed(kv)
    beside = swap(kv, 1)
    pairs = model // (BATCH * HEAD_DIM)
    block = ((pairs, 2 * rows, BATCH * rows), f32)
    lifted, weighted, stats = call(
        near_kernel,
        [block, block, ((pairs, 3, BATCH * rows), f32)],
        [me, queries[0], d_heads[0], beside, kv],
    )
    stats, turned = lax.optimization_barrier((stats, turned))
    turned = [turned[0], swap(turned[1], 2), swap(turned[2], 3)]
    d_across, far, kept = call(
        far_kernel,
        [half, ((pairs, rows, BATCH * rows), bf16), ((pairs, 2, BATCH * rows), f32)],
        [me, queries[0], d_heads[0], across, stats],
    )
    from_across = crossed(d_across)
    d_queries, d_beside, d_own = call(
        close_kernel,
        [((rows, model), bf16), half, partial],
        [queries[0], d_heads[0], beside, kv, across, lifted, weighted, kept, far],
    )
    d_beside, turned, upstream = lax.optimization_barrier((d_beside, turned, upstream))
    from_beside = swap(d_beside, 1)
    d_kv = (d_own + from_beside.astype(f32) + from_across.astype(f32)).astype(bf16)
    above = swap(d_kv, 2)
    d_beside = swap(d_kv, 1)
    grads = [d_kv, d_beside, above, swap(above, 1)]
    terms = call(
        terms_kernel,
        [((width, kv2), f32)] + [((width, kv2), bf16)] * (tall - 1),
        [me, lent, *turned, *grads],
    )
    order = [tall // 2, *range(1, tall // 2), *range(tall // 2 + 1, tall)]
    received = [swap(terms[delta], 4 * delta) for delta in order]
    near, lent = call(
        input_kernel,
        [((count // 2, rows, width), f32), ((count // 2, rows, width), bf16)],
        [d_kv, d_beside, *weights],
    )
    (grad_out,) = call(
        close_input_kernel,
        [((rows, model), bf16)],
        [me, saved, factor, upstream, near, swap(lent, 1)],
        [pltpu.VMEM((count, rows, width), f32)],
    )
    received, grad_out = lax.optimization_barrier((received, grad_out))
    total = terms[0]
    for part in received:
        total = total + part.astype(f32)
    weight_grad = total * (1.0 / math.sqrt(rows * count))
    return (grad_out[None], d_queries[None], weight_grad[None])


def solution(mesh):
    spec = P("pipe", "ctx", None)
    return jax.shard_map(
        per_device, mesh=mesh, in_specs=(spec,) * 5, out_specs=(spec,) * 3, check_vma=False
    )
```

```python
import functools
import math

import jax
import jax.numpy as jnp
from jax import lax
from jax.experimental import pallas as pl
from jax.experimental.pallas import tpu as pltpu
from jax.sharding import PartitionSpec as P

HEAD_DIM = 128
BATCH = 8
KV_HEADS = 2
EPSILON = 1e-06
NT = (((1,), (1,)), ((), ()))
VMEM = pl.BlockSpec(memory_space=pltpu.VMEM)
SMEM = pl.BlockSpec(memory_space=pltpu.SMEM)
PARAMS = pltpu.CompilerParams(vmem_limit_bytes=16 * 1024 * 1024)


def f32dot(a, b, dims=(((1,), (0,)), ((), ()))):
    return lax.dot_general(a, b, dims, preferred_element_type=jnp.float32)


def call(kernel, outs, args, scratch=()):
    in_specs = [SMEM if a.dtype == jnp.int32 else VMEM for a in args]
    return pl.pallas_call(
        kernel,
        out_shape=[jax.ShapeDtypeStruct(s, d) for s, d in outs],
        in_specs=in_specs,
        out_specs=[VMEM] * len(outs),
        scratch_shapes=list(scratch),
        compiler_params=PARAMS,
    )(*args)


def norm_kernel(me_ref, saved_ref, shard_ref, near_ref, lent_ref, t0_ref, t2_ref, t3_ref, factor_ref, copy_ref, held, held_t):
    copy_ref[...] = shard_ref[...]
    blocks, _, width = held.shape
    rest = me_ref[0] % 4
    wide = saved_ref[...].astype(jnp.float32)
    factor = lax.rsqrt(jnp.mean(wide * wide, axis=-1, keepdims=True) + EPSILON)
    factor_ref[...] = factor
    normed = (wide * factor).astype(jnp.bfloat16)
    for b in range(blocks):
        part = normed[:, b * width : (b + 1) * width]
        held[b] = part
        held_t[b] = part.T
    for zz in range(blocks // 4):
        for k in range(2):
            near_ref[k, zz] = held[zz * 4 + (rest ^ (2 * k))]
            lent_ref[k, zz] = held[zz * 4 + (rest ^ (2 * k + 1))]
        for d, ref in ((0, t0_ref), (2, t2_ref), (3, t3_ref)):
            ref[zz] = held_t[zz * 4 + (rest ^ d)]


def kv_kernel(me_ref, near_ref, lent_ref, *refs):
    weights, out_ref = refs[:-1], refs[-1]
    own = me_ref[0] // 4
    total = None
    for zz in range(len(weights) // 2):
        at = own ^ zz
        lhs = [jnp.concatenate([near_ref[k, at], lent_ref[k, at]], axis=0) for k in range(2)]
        rhs = jnp.concatenate([weights[2 * zz][...], weights[2 * zz + 1][...]], axis=0)
        part = f32dot(jnp.concatenate(lhs, axis=1), rhs)
        total = part if total is None else total + part
    out_ref[...] = total


def head_rows(ref, block, size):
    at = block * size * HEAD_DIM
    return jnp.concatenate([ref[:, at + h * HEAD_DIM : at + (h + 1) * HEAD_DIM] for h in range(size)], axis=0)


def reach(me_ref, rows, near):
    key_pos = lax.broadcasted_iota(jnp.int32, (rows, rows), 0)
    query_pos = lax.broadcasted_iota(jnp.int32, (rows, rows), 1)
    offset = (key_pos - query_pos) * (1 - 2 * (me_ref[0] % 2))
    return jnp.concatenate([offset <= 0 if near else offset >= 0] * BATCH, axis=1)


def columns(group):
    keys = slice(group * HEAD_DIM, (group + 1) * HEAD_DIM)
    return keys, slice(keys.start + KV_HEADS * HEAD_DIM, keys.stop + KV_HEADS * HEAD_DIM)


def near_kernel(me_ref, q_ref, g_ref, beside_ref, own_ref, lifted_ref, weighted_ref, stats_ref):
    rows = own_ref.shape[0]
    pairs = lifted_ref.shape[0]
    scale = math.log2(math.e) / math.sqrt(HEAD_DIM)
    mask = reach(me_ref, rows, True)
    for group in range(KV_HEADS):
        key_at, value_at = columns(group)
        keys = jnp.concatenate([beside_ref[:, key_at], own_ref[:, key_at]], axis=0)
        values = jnp.concatenate([beside_ref[:, value_at], own_ref[:, value_at]], axis=0)
        for pair in range(group * pairs // KV_HEADS, (group + 1) * pairs // KV_HEADS):
            scores = f32dot(keys, head_rows(q_ref, pair, BATCH), NT) * scale
            scores = jnp.concatenate([jnp.where(mask, scores[:rows], -1e30), scores[rows:]], axis=0)
            peak = jnp.max(scores, axis=0, keepdims=True)
            lifted = jnp.exp2(scores - peak)
            weighted = lifted * f32dot(values, head_rows(g_ref, pair, BATCH), NT)
            lifted_ref[pair] = lifted
            weighted_ref[pair] = weighted
            stats_ref[pair, 0:1] = peak
            stats_ref[pair, 1:2] = jnp.sum(lifted, axis=0, keepdims=True)
            stats_ref[pair, 2:3] = jnp.sum(weighted, axis=0, keepdims=True)


def far_kernel(me_ref, q_ref, g_ref, across_ref, stats_ref, owed_ref, d_scores_ref, rest_ref):
    rows = across_ref.shape[0]
    pairs = stats_ref.shape[0]
    scale = 1.0 / math.sqrt(HEAD_DIM)
    mask = reach(me_ref, rows, False)
    for group in range(KV_HEADS):
        key_at, value_at = columns(group)
        keys, values = across_ref[:, key_at], across_ref[:, value_at]
        d_keys = d_values = None
        for pair in range(group * pairs // KV_HEADS, (group + 1) * pairs // KV_HEADS):
            q, g = head_rows(q_ref, pair, BATCH), head_rows(g_ref, pair, BATCH)
            scores = f32dot(keys, q, NT) * (scale * math.log2(math.e))
            scores = jnp.where(mask, scores, -1e30)
            near_peak = stats_ref[pair, 0:1]
            peak = jnp.maximum(near_peak, jnp.max(scores, axis=0, keepdims=True))
            lifted = jnp.exp2(scores - peak)
            shrink = jnp.exp2(near_peak - peak)
            weighted = lifted * f32dot(values, g, NT)
            total = stats_ref[pair, 1:2] * shrink + jnp.sum(lifted, axis=0, keepdims=True)
            inverse = 1.0 / total
            row_dot = stats_ref[pair, 2:3] * shrink + jnp.sum(weighted, axis=0, keepdims=True)
            row_dot = row_dot * inverse
            d_scores = ((weighted - lifted * row_dot) * (inverse * scale)).astype(jnp.bfloat16)
            probs = (lifted * inverse).astype(jnp.bfloat16)
            dk, dv = f32dot(d_scores, q), f32dot(probs, g)
            d_keys = dk if d_keys is None else d_keys + dk
            d_values = dv if d_values is None else d_values + dv
            d_scores_ref[pair] = d_scores
            rest_ref[pair, 0:1] = shrink * inverse
            rest_ref[pair, 1:2] = row_dot
        owed_ref[:, key_at] = d_keys.astype(jnp.bfloat16)
        owed_ref[:, value_at] = d_values.astype(jnp.bfloat16)


def close_kernel(q_ref, g_ref, beside_ref, own_ref, across_ref, lifted_ref, weighted_ref, rest_ref, far_ref, dq_ref, db_ref, do_ref):
    rows = own_ref.shape[0]
    pairs = lifted_ref.shape[0]
    scale = 1.0 / math.sqrt(HEAD_DIM)
    for group in range(KV_HEADS):
        key_at, value_at = columns(group)
        keys = jnp.concatenate([r[:, key_at] for r in (beside_ref, own_ref, across_ref)], axis=0).T
        d_keys = d_values = None
        for pair in range(group * pairs // KV_HEADS, (group + 1) * pairs // KV_HEADS):
            lifted = lifted_ref[pair]
            part = rest_ref[pair, 0:1]
            d_scores = (weighted_ref[pair] - lifted * rest_ref[pair, 1:2]) * (part * scale)
            d_scores = d_scores.astype(jnp.bfloat16)
            probs = (lifted * part).astype(jnp.bfloat16)
            dk = f32dot(d_scores, head_rows(q_ref, pair, BATCH))
            dv = f32dot(probs, head_rows(g_ref, pair, BATCH))
            d_keys = dk if d_keys is None else d_keys + dk
            d_values = dv if d_values is None else d_values + dv
            dq = f32dot(keys, jnp.concatenate([d_scores, far_ref[pair]], axis=0)).astype(jnp.bfloat16)
            for h in range(BATCH):
                at = (BATCH * pair + h) * HEAD_DIM
                dq_ref[:, at : at + HEAD_DIM] = dq[:, h * rows : (h + 1) * rows].T
        for at, grad in ((key_at, d_keys), (value_at, d_values)):
            db_ref[:, at] = grad[:rows].astype(jnp.bfloat16)
            do_ref[:, at] = grad[rows:]


def terms_kernel(me_ref, lent_ref, *refs):
    turned, grads, outs = refs[:3], refs[3:7], refs[7:]
    own = me_ref[0] // 4
    d_kv = jnp.concatenate([r[...] for r in grads], axis=0)
    for delta, out_ref in enumerate(outs):
        at = own ^ delta
        lhs = jnp.concatenate([turned[0][at], lent_ref[0, at].T, turned[1][at], turned[2][at]], axis=1)
        out_ref[...] = f32dot(lhs, d_kv).astype(out_ref.dtype)


def input_kernel(own_ref, beside_ref, *refs):
    weights, near_ref, lent_ref = refs[:-2], refs[-2], refs[-1]
    rows, width = own_ref.shape[0], weights[0].shape[0]
    both = jnp.concatenate([own_ref[...], beside_ref[...]], axis=0)
    for half, weight in enumerate(weights):
        part = f32dot(both, weight[...], NT)
        near_ref[half] = part[:rows]
        lent_ref[half] = part[rows:].astype(jnp.bfloat16)


def close_input_kernel(me_ref, saved_ref, factor_ref, up_ref, near_ref, lent_ref, out_ref, held):
    blocks, rows, width = held.shape
    for half in range(blocks // 2):
        delta = half // 2 * 4 + half % 2 * 2
        held[me_ref[0] ^ delta] = near_ref[half]
        held[me_ref[0] ^ delta ^ 1] = lent_ref[half].astype(jnp.float32)
    factor = factor_ref[...]
    acc = jnp.zeros((rows, width), jnp.float32)
    for b in range(blocks):
        normed = saved_ref[:, b * width : (b + 1) * width].astype(jnp.float32) * factor
        acc = acc + held[b] * normed
    mean = jnp.sum(acc, axis=-1, keepdims=True) * (1.0 / (blocks * width))
    for b in range(blocks):
        at = slice(b * width, (b + 1) * width)
        normed = saved_ref[:, at].astype(jnp.float32) * factor
        grad = up_ref[:, at].astype(jnp.float32) + factor * (held[b] - normed * mean)
        out_ref[:, at] = grad.astype(jnp.bfloat16)


def swap(block, distance):
    count = lax.axis_size("ctx")
    return lax.ppermute(block, "ctx", [(i, i ^ distance) for i in range(count)])


def shifted(block, axis, distance):
    count = lax.axis_size(axis)
    return lax.ppermute(block, axis, [((i - distance) % count, i) for i in range(count)])


def crossed(block):
    count = lax.axis_size("ctx")
    route = [(i, (i + 1) % count if i % 2 else (i - 1) % count) for i in range(count)]
    return lax.ppermute(block, "ctx", route)


def passed(block):
    count = lax.axis_size("ctx")
    route = [(i, (i - 2) % count if i % 2 else (i + 2) % count) for i in range(count)]
    return lax.ppermute(block, "ctx", route)


def gathered(block, pieces):
    count = lax.axis_size("ctx")
    first = count // 2
    parts = {0: block, first: swap(block, first)}
    parts[2] = swap(block, 2)
    far = [0, first]
    step = first // 2
    while step >= 4:
        for d in list(far):
            parts[d ^ step] = swap(parts[d], step)
            far.append(d ^ step)
        step //= 2
    parts[4], pieces = lax.optimization_barrier((parts[4], pieces))
    parts[first], parts[2] = lax.optimization_barrier((parts[first], parts[2]))
    for d in far[1:]:
        direct = d & (first | 4) == first | 4 and first > 4
        parts[d ^ 2] = swap(parts[d ^ 4], 6) if direct else swap(parts[d], 2)
    return [parts[d] for d in range(0, count, 2)], pieces


def per_device(saved_in, grad_in, queries, d_heads, kv_weights):
    count = lax.axis_size("ctx")
    me = lax.axis_index("ctx").astype(jnp.int32).reshape(1)
    bf16, f32 = jnp.bfloat16, jnp.float32
    saved = saved_in[0]
    rows, model = saved.shape
    width, kv2 = kv_weights.shape[1:]
    tall = count // 4
    pieces = call(
        norm_kernel,
        [((2, tall, rows, width), bf16)] * 2 + [((tall, width, rows), bf16)] * 3 + [((rows, 1), f32), ((width, kv2), bf16)],
        [me, saved, kv_weights[0]],
        [pltpu.VMEM((count, rows, width), bf16), pltpu.VMEM((count, width, rows), bf16)],
    )
    weights, pieces = gathered(kv_weights[0], pieces)
    near, lent, *turned, factor, weights[0] = pieces
    lent = swap(lent, 1)
    weights[3], grad_in = lax.optimization_barrier((weights[3], grad_in))
    upstream = shifted(grad_in, "pipe", -1)[0]
    partial = ((rows, kv2), f32)
    half = ((rows, kv2), bf16)
    (both,) = call(kv_kernel, [((2 * rows, kv2), f32)], [me, near, lent, *weights])
    other = swap(both, 1)
    kv = (both[:rows] + other[rows:]).astype(bf16)
    beside = (both[rows:] + other[:rows]).astype(bf16)
    across = passed(beside)
    pairs = model // (BATCH * HEAD_DIM)
    block = ((pairs, 2 * rows, BATCH * rows), f32)
    lifted, weighted, stats = call(
        near_kernel,
        [block, block, ((pairs, 3, BATCH * rows), f32)],
        [me, queries[0], d_heads[0], beside, kv],
    )
    stats, turned = lax.optimization_barrier((stats, turned))
    turned = [turned[0], swap(turned[1], 2), swap(turned[2], 3)]
    d_across, far, kept = call(
        far_kernel,
        [half, ((pairs, rows, BATCH * rows), bf16), ((pairs, 2, BATCH * rows), f32)],
        [me, queries[0], d_heads[0], across, stats],
    )
    from_across = crossed(d_across)
    d_queries, d_beside, d_own = call(
        close_kernel,
        [((rows, model), bf16), half, partial],
        [queries[0], d_heads[0], beside, kv, across, lifted, weighted, kept, far],
    )
    d_beside, turned = lax.optimization_barrier((d_beside, turned))
    from_across, upstream = lax.optimization_barrier((from_across, upstream))
    from_beside = swap(d_beside, 1)
    d_kv = (d_own + from_beside.astype(f32) + from_across.astype(f32)).astype(bf16)
    above = swap(d_kv, 2)
    d_beside = swap(d_kv, 1)
    grads = [d_kv, d_beside, above, swap(above, 1)]
    terms = call(
        terms_kernel,
        [((width, kv2), f32)] + [((width, kv2), bf16)] * (tall - 1),
        [me, lent, *turned, *grads],
    )
    order = [tall // 2, *range(1, tall // 2), *range(tall // 2 + 1, tall)]
    received = [swap(terms[delta], 4 * delta) for delta in order]
    near, lent = call(
        input_kernel,
        [((count // 2, rows, width), f32), ((count // 2, rows, width), bf16)],
        [d_kv, d_beside, *weights],
    )
    (grad_out,) = call(
        close_input_kernel,
        [((rows, model), bf16)],
        [me, saved, factor, upstream, near, swap(lent, 1)],
        [pltpu.VMEM((count, rows, width), f32)],
    )
    received, grad_out = lax.optimization_barrier((received, grad_out))
    total = terms[0]
    for part in received:
        total = total + part.astype(f32)
    weight_grad = total * (1.0 / math.sqrt(rows * count))
    return (grad_out[None], d_queries[None], weight_grad[None])


def solution(mesh):
    spec = P("pipe", "ctx", None)
    return jax.shard_map(
        per_device, mesh=mesh, in_specs=(spec,) * 5, out_specs=(spec,) * 3, check_vma=False
    )
```

```python
import functools
import math

import jax
import jax.numpy as jnp
from jax import lax
from jax.experimental import pallas as pl
from jax.experimental.pallas import tpu as pltpu
from jax.sharding import PartitionSpec as P

HEAD_DIM = 128
BATCH = 8
KV_HEADS = 2
EPSILON = 1e-06
NT = (((1,), (1,)), ((), ()))
VMEM = pl.BlockSpec(memory_space=pltpu.VMEM)
SMEM = pl.BlockSpec(memory_space=pltpu.SMEM)
PARAMS = pltpu.CompilerParams(vmem_limit_bytes=16 * 1024 * 1024)


def f32dot(a, b, dims=(((1,), (0,)), ((), ()))):
    return lax.dot_general(a, b, dims, preferred_element_type=jnp.float32)


def call(kernel, outs, args, scratch=()):
    in_specs = [SMEM if a.dtype == jnp.int32 else VMEM for a in args]
    return pl.pallas_call(
        kernel,
        out_shape=[jax.ShapeDtypeStruct(s, d) for s, d in outs],
        in_specs=in_specs,
        out_specs=[VMEM] * len(outs),
        scratch_shapes=list(scratch),
        compiler_params=PARAMS,
    )(*args)


def norm_kernel(me_ref, saved_ref, shard_ref, near_ref, lent_ref, t0_ref, t2_ref, t3_ref, factor_ref, copy_ref, held, held_t):
    copy_ref[...] = shard_ref[...]
    blocks, _, width = held.shape
    rest = me_ref[0] % 4
    wide = saved_ref[...].astype(jnp.float32)
    factor = lax.rsqrt(jnp.mean(wide * wide, axis=-1, keepdims=True) + EPSILON)
    factor_ref[...] = factor
    normed = (wide * factor).astype(jnp.bfloat16)
    for b in range(blocks):
        part = normed[:, b * width : (b + 1) * width]
        held[b] = part
        held_t[b] = part.T
    for zz in range(blocks // 4):
        for k in range(2):
            near_ref[k, zz] = held[zz * 4 + (rest ^ (2 * k))]
            lent_ref[k, zz] = held[zz * 4 + (rest ^ (2 * k + 1))]
        for d, ref in ((0, t0_ref), (2, t2_ref), (3, t3_ref)):
            ref[zz] = held_t[zz * 4 + (rest ^ d)]


def kv_kernel(me_ref, near_ref, lent_ref, *refs):
    weights, out_ref = refs[:-1], refs[-1]
    own = me_ref[0] // 4
    total = None
    for zz in range(len(weights) // 2):
        at = own ^ zz
        lhs = [jnp.concatenate([near_ref[k, at], lent_ref[k, at]], axis=0) for k in range(2)]
        rhs = jnp.concatenate([weights[2 * zz][...], weights[2 * zz + 1][...]], axis=0)
        part = f32dot(jnp.concatenate(lhs, axis=1), rhs)
        total = part if total is None else total + part
    out_ref[...] = total


def head_rows(ref, block, size):
    at = block * size * HEAD_DIM
    return jnp.concatenate([ref[:, at + h * HEAD_DIM : at + (h + 1) * HEAD_DIM] for h in range(size)], axis=0)


def reach(me_ref, rows, near):
    key_pos = lax.broadcasted_iota(jnp.int32, (rows, rows), 0)
    query_pos = lax.broadcasted_iota(jnp.int32, (rows, rows), 1)
    offset = (key_pos - query_pos) * (1 - 2 * (me_ref[0] % 2))
    return jnp.concatenate([offset <= 0 if near else offset >= 0] * BATCH, axis=1)


def columns(group):
    keys = slice(group * HEAD_DIM, (group + 1) * HEAD_DIM)
    return keys, slice(keys.start + KV_HEADS * HEAD_DIM, keys.stop + KV_HEADS * HEAD_DIM)


def near_kernel(me_ref, q_ref, g_ref, beside_ref, own_ref, lifted_ref, weighted_ref, stats_ref):
    rows = own_ref.shape[0]
    pairs = lifted_ref.shape[0]
    scale = math.log2(math.e) / math.sqrt(HEAD_DIM)
    mask = reach(me_ref, rows, True)
    for group in range(KV_HEADS):
        key_at, value_at = columns(group)
        keys = jnp.concatenate([beside_ref[:, key_at], own_ref[:, key_at]], axis=0)
        values = jnp.concatenate([beside_ref[:, value_at], own_ref[:, value_at]], axis=0)
        for pair in range(group * pairs // KV_HEADS, (group + 1) * pairs // KV_HEADS):
            scores = f32dot(keys, head_rows(q_ref, pair, BATCH), NT) * scale
            scores = jnp.concatenate([jnp.where(mask, scores[:rows], -1e30), scores[rows:]], axis=0)
            peak = jnp.max(scores, axis=0, keepdims=True)
            lifted = jnp.exp2(scores - peak)
            weighted = lifted * f32dot(values, head_rows(g_ref, pair, BATCH), NT)
            lifted_ref[pair] = lifted
            weighted_ref[pair] = weighted
            stats_ref[pair, 0:1] = peak
            stats_ref[pair, 1:2] = jnp.sum(lifted, axis=0, keepdims=True)
            stats_ref[pair, 2:3] = jnp.sum(weighted, axis=0, keepdims=True)


def far_kernel(me_ref, q_ref, g_ref, across_ref, stats_ref, owed_ref, d_scores_ref, rest_ref):
    rows = across_ref.shape[0]
    pairs = stats_ref.shape[0]
    scale = 1.0 / math.sqrt(HEAD_DIM)
    mask = reach(me_ref, rows, False)
    for group in range(KV_HEADS):
        key_at, value_at = columns(group)
        keys, values = across_ref[:, key_at], across_ref[:, value_at]
        d_keys = d_values = None
        for pair in range(group * pairs // KV_HEADS, (group + 1) * pairs // KV_HEADS):
            q, g = head_rows(q_ref, pair, BATCH), head_rows(g_ref, pair, BATCH)
            scores = f32dot(keys, q, NT) * (scale * math.log2(math.e))
            scores = jnp.where(mask, scores, -1e30)
            near_peak = stats_ref[pair, 0:1]
            peak = jnp.maximum(near_peak, jnp.max(scores, axis=0, keepdims=True))
            lifted = jnp.exp2(scores - peak)
            shrink = jnp.exp2(near_peak - peak)
            weighted = lifted * f32dot(values, g, NT)
            total = stats_ref[pair, 1:2] * shrink + jnp.sum(lifted, axis=0, keepdims=True)
            inverse = 1.0 / total
            row_dot = stats_ref[pair, 2:3] * shrink + jnp.sum(weighted, axis=0, keepdims=True)
            row_dot = row_dot * inverse
            d_scores = ((weighted - lifted * row_dot) * (inverse * scale)).astype(jnp.bfloat16)
            probs = (lifted * inverse).astype(jnp.bfloat16)
            dk, dv = f32dot(d_scores, q), f32dot(probs, g)
            d_keys = dk if d_keys is None else d_keys + dk
            d_values = dv if d_values is None else d_values + dv
            d_scores_ref[pair] = d_scores
            rest_ref[pair, 0:1] = shrink * inverse
            rest_ref[pair, 1:2] = row_dot
        owed_ref[:, key_at] = d_keys.astype(jnp.bfloat16)
        owed_ref[:, value_at] = d_values.astype(jnp.bfloat16)


def close_kernel(q_ref, g_ref, beside_ref, own_ref, across_ref, lifted_ref, weighted_ref, rest_ref, far_ref, dq_ref, db_ref, do_ref):
    rows = own_ref.shape[0]
    pairs = lifted_ref.shape[0]
    scale = 1.0 / math.sqrt(HEAD_DIM)
    for group in range(KV_HEADS):
        key_at, value_at = columns(group)
        keys = jnp.concatenate([r[:, key_at] for r in (beside_ref, own_ref, across_ref)], axis=0).T
        d_keys = d_values = None
        for pair in range(group * pairs // KV_HEADS, (group + 1) * pairs // KV_HEADS):
            lifted = lifted_ref[pair]
            part = rest_ref[pair, 0:1]
            d_scores = (weighted_ref[pair] - lifted * rest_ref[pair, 1:2]) * (part * scale)
            d_scores = d_scores.astype(jnp.bfloat16)
            probs = (lifted * part).astype(jnp.bfloat16)
            dk = f32dot(d_scores, head_rows(q_ref, pair, BATCH))
            dv = f32dot(probs, head_rows(g_ref, pair, BATCH))
            d_keys = dk if d_keys is None else d_keys + dk
            d_values = dv if d_values is None else d_values + dv
            dq = f32dot(keys, jnp.concatenate([d_scores, far_ref[pair]], axis=0)).astype(jnp.bfloat16)
            for h in range(BATCH):
                at = (BATCH * pair + h) * HEAD_DIM
                dq_ref[:, at : at + HEAD_DIM] = dq[:, h * rows : (h + 1) * rows].T
        for at, grad in ((key_at, d_keys), (value_at, d_values)):
            db_ref[:, at] = grad[:rows].astype(jnp.bfloat16)
            do_ref[:, at] = grad[rows:]


def terms_kernel(me_ref, lent_ref, *refs):
    turned, grads, outs = refs[:3], refs[3:7], refs[7:]
    own = me_ref[0] // 4
    d_kv = jnp.concatenate([r[...] for r in grads], axis=0)
    for delta, out_ref in enumerate(outs):
        at = own ^ delta
        lhs = jnp.concatenate([turned[0][at], lent_ref[0, at].T, turned[1][at], turned[2][at]], axis=1)
        out_ref[...] = f32dot(lhs, d_kv).astype(out_ref.dtype)


def input_kernel(own_ref, beside_ref, *refs):
    weights, near_ref, lent_ref = refs[:-2], refs[-2], refs[-1]
    rows, width = own_ref.shape[0], weights[0].shape[0]
    both = jnp.concatenate([own_ref[...], beside_ref[...]], axis=0)
    for half, weight in enumerate(weights):
        part = f32dot(both, weight[...], NT)
        near_ref[half] = part[:rows]
        lent_ref[half] = part[rows:].astype(jnp.bfloat16)


def close_input_kernel(me_ref, saved_ref, factor_ref, up_ref, near_ref, lent_ref, out_ref, held):
    blocks, rows, width = held.shape
    for half in range(blocks // 2):
        delta = half // 2 * 4 + half % 2 * 2
        held[me_ref[0] ^ delta] = near_ref[half]
        held[me_ref[0] ^ delta ^ 1] = lent_ref[half].astype(jnp.float32)
    factor = factor_ref[...]
    acc = jnp.zeros((rows, width), jnp.float32)
    for b in range(blocks):
        normed = saved_ref[:, b * width : (b + 1) * width].astype(jnp.float32) * factor
        acc = acc + held[b] * normed
    mean = jnp.sum(acc, axis=-1, keepdims=True) * (1.0 / (blocks * width))
    for b in range(blocks):
        at = slice(b * width, (b + 1) * width)
        normed = saved_ref[:, at].astype(jnp.float32) * factor
        grad = up_ref[:, at].astype(jnp.float32) + factor * (held[b] - normed * mean)
        out_ref[:, at] = grad.astype(jnp.bfloat16)


def swap(block, distance):
    count = lax.axis_size("ctx")
    return lax.ppermute(block, "ctx", [(i, i ^ distance) for i in range(count)])


def shifted(block, axis, distance):
    count = lax.axis_size(axis)
    return lax.ppermute(block, axis, [((i - distance) % count, i) for i in range(count)])


def crossed(block):
    count = lax.axis_size("ctx")
    route = [(i, (i + 1) % count if i % 2 else (i - 1) % count) for i in range(count)]
    return lax.ppermute(block, "ctx", route)


def passed(block):
    count = lax.axis_size("ctx")
    route = [(i, (i - 2) % count if i % 2 else (i + 2) % count) for i in range(count)]
    return lax.ppermute(block, "ctx", route)


def gathered(block, pieces):
    count = lax.axis_size("ctx")
    first = count // 2
    parts = {0: block, first: swap(block, first)}
    parts[2] = swap(block, 2)
    far = [0, first]
    step = first // 2
    while step >= 4:
        for d in list(far):
            parts[d ^ step] = swap(parts[d], step)
            far.append(d ^ step)
        step //= 2
    parts[4], pieces = lax.optimization_barrier((parts[4], pieces))
    parts[first], parts[2] = lax.optimization_barrier((parts[first], parts[2]))
    for d in far[1:]:
        direct = d & (first | 4) == first | 4 and first > 4
        parts[d ^ 2] = swap(parts[d ^ 4], 6) if direct else swap(parts[d], 2)
    return [parts[d] for d in range(0, count, 2)], pieces


def per_device(saved_in, grad_in, queries, d_heads, kv_weights):
    count = lax.axis_size("ctx")
    me = lax.axis_index("ctx").astype(jnp.int32).reshape(1)
    bf16, f32 = jnp.bfloat16, jnp.float32
    saved = saved_in[0]
    rows, model = saved.shape
    width, kv2 = kv_weights.shape[1:]
    tall = count // 4
    pieces = call(
        norm_kernel,
        [((2, tall, rows, width), bf16)] * 2 + [((tall, width, rows), bf16)] * 3 + [((rows, 1), f32), ((width, kv2), bf16)],
        [me, saved, kv_weights[0]],
        [pltpu.VMEM((count, rows, width), bf16), pltpu.VMEM((count, width, rows), bf16)],
    )
    weights, pieces = gathered(kv_weights[0], pieces)
    near, lent, *turned, factor, weights[0] = pieces
    lent = swap(lent, 1)
    weights[3], grad_in = lax.optimization_barrier((weights[3], grad_in))
    upstream = shifted(grad_in, "pipe", -1)[0]
    partial = ((rows, kv2), f32)
    half = ((rows, kv2), bf16)
    (both,) = call(kv_kernel, [((2 * rows, kv2), f32)], [me, near, lent, *weights])
    other = swap(both, 1)
    kv = (both[:rows] + other[rows:]).astype(bf16)
    beside = (both[rows:] + other[:rows]).astype(bf16)
    across = passed(beside)
    pairs = model // (BATCH * HEAD_DIM)
    block = ((pairs, 2 * rows, BATCH * rows), f32)
    lifted, weighted, stats = call(
        near_kernel,
        [block, block, ((pairs, 3, BATCH * rows), f32)],
        [me, queries[0], d_heads[0], beside, kv],
    )
    stats, turned = lax.optimization_barrier((stats, turned))
    diagonal = swap(turned[2], 3)
    turned = [turned[0], swap(turned[1], 2), diagonal]
    d_across, far, kept = call(
        far_kernel,
        [half, ((pairs, rows, BATCH * rows), bf16), ((pairs, 2, BATCH * rows), f32)],
        [me, queries[0], d_heads[0], across, stats],
    )
    from_across = crossed(d_across)
    d_queries, d_beside, d_own = call(
        close_kernel,
        [((rows, model), bf16), half, partial],
        [queries[0], d_heads[0], beside, kv, across, lifted, weighted, kept, far],
    )
    d_beside, turned = lax.optimization_barrier((d_beside, turned))
    from_across, upstream = lax.optimization_barrier((from_across, upstream))
    from_beside = swap(d_beside, 1)
    d_kv = (d_own + from_beside.astype(f32) + from_across.astype(f32)).astype(bf16)
    above = swap(d_kv, 2)
    d_beside = swap(d_kv, 1)
    grads = [d_kv, d_beside, above, swap(above, 1)]
    terms = call(
        terms_kernel,
        [((width, kv2), f32)] + [((width, kv2), bf16)] * (tall - 1),
        [me, lent, *turned, *grads],
    )
    order = [tall // 2, *range(1, tall // 2), *range(tall // 2 + 1, tall)]
    received = [swap(terms[delta], 4 * delta) for delta in order]
    near, lent = call(
        input_kernel,
        [((count // 2, rows, width), f32), ((count // 2, rows, width), bf16)],
        [d_kv, d_beside, *weights],
    )
    (grad_out,) = call(
        close_input_kernel,
        [((rows, model), bf16)],
        [me, saved, factor, upstream, near, swap(lent, 1)],
        [pltpu.VMEM((count, rows, width), f32)],
    )
    received, grad_out = lax.optimization_barrier((received, grad_out))
    total = terms[0]
    for part in received:
        total = total + part.astype(f32)
    weight_grad = total * (1.0 / math.sqrt(rows * count))
    return (grad_out[None], d_queries[None], weight_grad[None])


def solution(mesh):
    spec = P("pipe", "ctx", None)
    return jax.shard_map(
        per_device, mesh=mesh, in_specs=(spec,) * 5, out_specs=(spec,) * 3, check_vma=False
    )
```
